128 devices in a mesh: dp: 4 (over z), seq: 32 (over y, x, core).
Axes of the slice: x: 4, y: 4, z: 4, core: 2. Of those that a mesh axis runs over, the one named last changes fastest.
Arguments:
- queries: bfloat16 [16384, 4096], P(('dp', 'seq')), parts along dimension 0, may hold values from -7 to 7
- key_vectors: bfloat16 [16384, 512], P(('dp', 'seq')), parts along dimension 0, may hold values from -6 to 6
- value_vectors: bfloat16 [16384, 512], P(('dp', 'seq')), parts along dimension 0, may hold values from -12 to 12
- residual: bfloat16 [16384, 2048], P(('dp', 'seq')), parts along dimension 0, may hold values from -16 to 16
- out_weight: bfloat16 [4096, 2048], P('seq'), may hold values from -0.09375 to 0.09375
- norm_gain: float32 [2048], replicated, may hold values from 0.1 to 1.9
- routes: int32 [16384, 8], P(('dp', 'seq')), parts along dimension 0, may hold values from 0 to 63, all different within a row; in each aligned block of 128 rows (0 to 127, 128 to 255, ...) at most 24 rows name the same one
- route_gates: float32 [16384, 8], P(('dp', 'seq')), parts along dimension 0, may hold values from 0.05 to 1
- w_gate: bfloat16 [64, 2048, 768], P('seq'), may hold values from -0.125 to 0.125
- w_up: bfloat16 [64, 2048, 768], P('seq'), may hold values from -0.125 to 0.125
- w_down: bfloat16 [64, 768, 2048], P('seq'), may hold values from -0.21875 to 0.21875
Outputs:
- stream: bfloat16 [16384, 2048], P(('dp', 'seq')), parts along dimension 0
- layer_out: bfloat16 [16384, 2048], P(('dp', 'seq')), parts along dimension 0
The draws below stay inside these ranges and needn't reach their ends.
There are 4 independent parts, one for each index of `dp`. The reference program is written for one: setup_inputs(seed, part) draws one part's arguments, and reference() takes and returns one part's arrays. A program takes and returns all parts, laid end to end along the dimension named above; an argument that names none is the same for every part. Nothing has to cross between parts.
Inputs may be any that keep to these rules, and one draw needn't show every extreme that they name: `routes`: each token names 8 different experts; among the 128 tokens of one device no expert is named more than 24 times.
All inputs are finite; a program needn't handle non-finite values.
Results may differ from the reference program's by a relative error of at most 0.019.
Values may be sent and summed in bfloat16 or wider, within the bound.
No kernel may reach another device: no remote copies, remote signals or barrier semaphores. Data moves between devices by JAX's collectives and lax.ppermute only.
A program may use at most 128 MiB of HBM per device.

```python
import math
import jax
import jax.numpy as jnp
import numpy as np
from jax import lax

D = 2048
FF = 768
HEADS = 32
KV_HEADS = 4
HEAD_DIM = 128
TOPK = 8
TOK_DEV = 128
TOKENS = 4096
EXPERTS = 64
CAP = 24
N_SEQ = 32


def draw_queries(key, part):
    key = jax.random.fold_in(key, 11)
    values_base = jnp.clip(jax.random.normal(key, (TOKENS, HEADS, HEAD_DIM), jnp.float32), -6.0, 6.0)
    return values_base.reshape(TOKENS, HEADS * HEAD_DIM).astype(jnp.bfloat16)


def draw_key_vectors(key, part):
    key = jax.random.fold_in(key, 12)
    values_base = jnp.clip(jax.random.normal(key, (TOKENS, KV_HEADS, HEAD_DIM), jnp.float32), -6.0, 6.0)
    return values_base.reshape(TOKENS, KV_HEADS * HEAD_DIM).astype(jnp.bfloat16)


def draw_residual(key, part):
    key = jax.random.fold_in(key, 13)
    subkeys = jax.random.split(key, 3)
    row_scale = jnp.exp(jax.random.uniform(subkeys[0], (TOKENS, 1), jnp.float32, math.log(0.2), math.log(2.0)))
    col_scale = jnp.exp(jax.random.uniform(subkeys[1], (1, D), jnp.float32, math.log(0.2), math.log(2.0)))
    noise_draw = jnp.clip(jax.random.normal(subkeys[2], (TOKENS, D), jnp.float32), -4.0, 4.0)
    return (row_scale * col_scale * noise_draw).astype(jnp.bfloat16)


def levels(rng, shape, cuts, least, largest):
    gain, own = 1.0, jax.random.fold_in(rng, 6)
    for axis_at, shards_of in cuts:
        steps = jnp.exp(jax.random.uniform(jax.random.fold_in(own, axis_at), (shards_of,), jnp.float32, least / len(cuts), largest / len(cuts)))
        gain = gain * jnp.repeat(steps, shape[axis_at] // shards_of).reshape([-1 if axis == axis_at else 1 for axis in range(len(shape))])
    return gain


def routed_block(key, own, number, rows, number_of, top, bound, skew):
    order = jax.random.permutation(key, number_of)
    crowded, common = portions_of(number_of, rows * top, bound, skew, True), portions_of(number_of, rows * top, bound, skew, False)
    places = jnp.arange(number_of)

    def named(lengths, rotation):
        used = int((lengths > 0).sum())
        fixed = max(1, used // 4)
        passed = fixed + (places - fixed + rotation * (used - fixed)) % max(1, number_of - fixed)
        return jnp.zeros((number_of,), jnp.int32).at[order[jnp.where(places < fixed, places, passed)]].set(jnp.asarray(lengths, jnp.int32))

    lengths = jnp.where(number % 4 == 0, named(crowded, number // 4), named(common, number - number // 4 - 1))
    mixed = jax.random.permutation(jax.random.fold_in(own, 3), number_of)
    donor, taker = mixed[0:number_of // 2 * 2:2], mixed[1:number_of // 2 * 2:2]
    room = jnp.minimum(lengths[donor] - 1, bound - lengths[taker]) // 2
    room = jnp.where((donor == order[0]) | (taker == order[0]) | (lengths[taker] == 0), 0, jnp.maximum(room, 0))
    passed = jax.random.randint(jax.random.fold_in(own, 4), (number_of // 2,), 0, 1 << 20) % (room + 1)
    lengths = lengths.at[donor].add(-passed).at[taker].add(passed)
    items = jnp.searchsorted(jnp.cumsum(lengths), jnp.arange(rows * top), side="right").astype(jnp.int32)
    table = items.reshape(top, rows).T
    table = table[jax.random.permutation(jax.random.fold_in(own, 1), rows)]
    rotation = jax.random.randint(jax.random.fold_in(own, 2), (rows, 1), 0, top)
    return jnp.take_along_axis(table, (jnp.arange(top)[None, :] + rotation) % top, axis=1)


def portions_of(amount, total, bound, slope, full):
    loads = [(1 << 20) // math.isqrt(grade ** slope) + 1 for grade in range(1, amount + 1)]
    largest = bound if full else min(bound, max(-(-total // amount), total * loads[0] // sum(loads)))
    least = 1 if total - largest >= amount - 1 else 0
    counts, spare = [largest] + [least] * (amount - 1), total - largest - least * (amount - 1)
    while spare > 0:
        candidates = [i for i in range(1, amount) if counts[i] < largest] or [i for i in range(1, amount) if counts[i] < bound]
        whole, left = sum([loads[i] for i in candidates]), spare
        for i in candidates:
            more = min(bound - counts[i], max(1, left * loads[i] // whole), spare)
            counts[i] = counts[i] + more
            spare = spare - more
    return np.array(counts)


def centred(stream_key, extent, width, bound, cuts=(), kind=jnp.bfloat16):
    values = jax.random.normal(stream_key, extent, jnp.float32) * width
    if len(cuts) > 0:
        values = levels(stream_key, extent, cuts, -0.22, 0.18) * values
    return jnp.clip(values, min=-bound, max=bound).astype(kind)


def setup_inputs(seed: int = 0, part: int = 0) -> dict:
    arg_keys = jax.random.split(jax.random.key(seed), 12)
    own_keys = jax.random.split(jax.random.fold_in(arg_keys[11], part), 12)
    queries = draw_queries(jax.random.fold_in(jax.random.fold_in(arg_keys[11], part), 71), part)
    key_vectors = draw_key_vectors(jax.random.fold_in(jax.random.fold_in(arg_keys[11], part), 71), part)
    value_vectors = centred(own_keys[2], (TOKENS, KV_HEADS * HEAD_DIM), 3.0, 12.0, ((0, 32),))
    residual = draw_residual(jax.random.fold_in(jax.random.fold_in(arg_keys[11], part), 71), part)
    out_weight = centred(arg_keys[4], (HEADS * HEAD_DIM, D), (HEADS * HEAD_DIM) ** -0.5, 0.09375, ((0, 32),))
    norm_gain = jnp.clip(1.0 + 0.18 * jax.random.normal(arg_keys[5], (D,), jnp.float32), 0.1, 1.9)
    routes_keys = jax.random.split(jax.random.fold_in(own_keys[6], 1), TOKENS // TOK_DEV)
    routes_turns = jax.random.permutation(jax.random.fold_in(own_keys[6], 3), TOKENS // TOK_DEV)
    routes = jax.vmap(lambda own, number: routed_block(jax.random.fold_in(own_keys[6], 2), own, number, TOK_DEV, EXPERTS, TOPK, CAP, 2))(routes_keys, routes_turns).reshape((TOKENS, TOPK))
    route_gates = jnp.clip(jnp.exp(math.log(1.0) - 2.9957323 * jax.random.uniform(own_keys[7], (TOKENS, TOPK), jnp.float32) ** levels(own_keys[7], (TOKENS, TOPK), ((0, 32),), -0.2, 0.2)), 0.05, 1.0)
    w_gate = centred(arg_keys[8], (EXPERTS, D, FF), D ** -0.5, 0.125, ((0, 32),))
    w_up = centred(arg_keys[9], (EXPERTS, D, FF), D ** -0.5, 0.125, ((0, 32),))
    w_down = centred(arg_keys[10], (EXPERTS, FF, D), FF ** -0.5, 0.21875, ((0, 32),))
    return {"queries": queries, "key_vectors": key_vectors, "value_vectors": value_vectors, "residual": residual, "out_weight": out_weight, "norm_gain": norm_gain, "routes": routes, "route_gates": route_gates, "w_gate": w_gate, "w_up": w_up, "w_down": w_down}


def reference(queries, key_vectors, value_vectors, residual, out_weight, norm_gain, routes, route_gates, w_gate, w_up, w_down):
    score_scale = HEAD_DIM ** (-0.5)
    q_heads = queries.reshape(TOKENS, HEADS, HEAD_DIM).transpose(1, 0, 2).astype(jnp.float32)
    k_heads = key_vectors.reshape(TOKENS, KV_HEADS, HEAD_DIM).transpose(1, 0, 2).astype(jnp.float32)
    v_heads = value_vectors.reshape(TOKENS, KV_HEADS, HEAD_DIM).transpose(1, 0, 2).astype(jnp.float32)
    group_size = HEADS // KV_HEADS
    position = jnp.arange(TOKENS, dtype=jnp.int32)
    causal = position[None, :] <= position[:, None]

    def one_head(head_index):
        group_index = head_index // group_size
        scores = jnp.dot(q_heads[head_index], k_heads[group_index].T, preferred_element_type=jnp.float32) * score_scale
        scores = jnp.where(causal, scores, -1e+30)
        row_max = lax.optimization_barrier(jnp.max(scores, axis=1, keepdims=True))
        weight = jnp.exp(scores - row_max)
        probs = (weight / lax.optimization_barrier(jnp.sum(weight, axis=1, keepdims=True))).astype(jnp.bfloat16)
        return jnp.dot(probs.astype(jnp.float32), v_heads[group_index], preferred_element_type=jnp.float32).astype(jnp.bfloat16)
    per_head = lax.map(one_head, jnp.arange(HEADS, dtype=jnp.int32))
    attended = per_head.transpose(1, 0, 2).reshape(TOKENS, HEADS * HEAD_DIM)
    group_width = HEADS * HEAD_DIM // N_SEQ

    def add_group(running, group_index):
        start = (group_index * group_width).astype(jnp.int32)
        cols_part = lax.dynamic_slice_in_dim(attended, start, group_width, 1).astype(jnp.float32)
        rows_part = lax.dynamic_slice_in_dim(out_weight, start, group_width, 0).astype(jnp.float32)
        partial_sum = jnp.dot(cols_part, rows_part, preferred_element_type=jnp.float32).astype(jnp.bfloat16)
        return (running + partial_sum.astype(jnp.float32), None)
    attn_sum, _ = lax.scan(add_group, jnp.zeros((TOKENS, D), jnp.float32), jnp.arange(N_SEQ, dtype=jnp.int32))
    stream = (residual.astype(jnp.float32) + attn_sum).astype(jnp.bfloat16)
    stream_f = stream.astype(jnp.float32)
    normed = (stream_f * lax.rsqrt(lax.optimization_barrier(jnp.mean(stream_f * stream_f, axis=1, keepdims=True)) + 1e-06) * norm_gain.astype(jnp.float32)).astype(jnp.bfloat16)
    route_share = route_gates / lax.optimization_barrier(jnp.sum(route_gates, axis=1, keepdims=True))
    flat_routes = routes.reshape(-1).astype(jnp.int32)
    expert_hits = (flat_routes[:, None] == jnp.arange(EXPERTS, dtype=jnp.int32)[None, :]).astype(jnp.int32)
    slot_rank = lax.optimization_barrier(jnp.sum((jnp.cumsum(expert_hits, axis=0) - 1) * expert_hits, axis=1)).astype(jnp.int32)
    room = N_SEQ * CAP
    owner_token = (jnp.arange(TOKENS * TOPK, dtype=jnp.int32) // TOPK).astype(jnp.int32)
    slot_table = jnp.full((EXPERTS, room), TOKENS, jnp.int32).at[flat_routes, slot_rank].set(owner_token)
    padded = jnp.concatenate([normed, jnp.zeros((1, D), normed.dtype)], axis=0)

    def one_expert(expert_index):
        picked_rows = padded[slot_table[expert_index]].astype(jnp.float32)
        gate_part = jnp.dot(picked_rows, w_gate[expert_index].astype(jnp.float32), preferred_element_type=jnp.float32)
        up_part = jnp.dot(picked_rows, w_up[expert_index].astype(jnp.float32), preferred_element_type=jnp.float32)
        hidden = (jax.nn.silu(gate_part) * up_part).astype(jnp.bfloat16)
        return jnp.dot(hidden.astype(jnp.float32), w_down[expert_index].astype(jnp.float32), preferred_element_type=jnp.float32).astype(jnp.bfloat16)
    expert_rows = lax.map(one_expert, jnp.arange(EXPERTS, dtype=jnp.int32))
    routed = expert_rows[flat_routes, slot_rank].reshape(TOKENS, TOPK, D).astype(jnp.float32)
    expert_sum = jnp.einsum('trd,tr->td', routed, route_share.astype(jnp.float32))
    layer_out = (stream_f + expert_sum).astype(jnp.bfloat16)
    return (stream, layer_out)
```

```python
import functools

import jax
import jax.numpy as jnp
from jax import lax
from jax.experimental import pallas as pl
from jax.experimental.pallas import tpu as pltpu
from jax.sharding import PartitionSpec as P

HEADS = 32
KV_HEADS = 4
HEAD_DIM = 128
TOPK = 8
SIDE = 4
CHIPS = SIDE * SIDE
CORES = 2
OFFSETS = (0, -1, 1, 2)
TOLD_ROWS = 32
LOG2E = 1.4426950408889634
ANY = pl.BlockSpec(memory_space=pl.ANY)
VMEM_LIMIT = 60 * 1024 * 1024


def pairs_of(dy, dx, swap):
    pairs = []
    for y in range(SIDE):
        for x in range(SIDE):
            for c in range(CORES):
                source = (y * SIDE + x) * CORES + c
                target = ((y + dy) % SIDE * SIDE + (x + dx) % SIDE) * CORES + (c ^ swap)
                pairs.append((source, target))
    return pairs


def along(value, axis, step):
    dy, dx = (step, 0) if axis == "y" else (0, step)
    return lax.ppermute(value, "seq", pairs_of(dy, dx, 0))


def to_sibling(value):
    return lax.ppermute(value, "seq", pairs_of(0, 0, 1))


def together(*values):
    return lax.optimization_barrier(values)


def near(a, b):
    a, b = together(a, b)
    got = [along(value, axis, step) for value, axis in ((a, "x"), (b, "y")) for step in (1, -1, 2)]
    got = together(*got)
    return together(
        jnp.concatenate([a, *got[:3]], axis=0), jnp.concatenate([b, *got[3:]], axis=0)
    )


def wide(a, b, beside):
    got = (along(a, "y", 1), along(a, "y", -1), along(b, "x", 1), along(b, "x", -1))
    return together(*got, *beside())


def wide_far(a, b, got, beside):
    ab, aa, bb, ba = got
    half_a, half_b = a.shape[0] // 2, b.shape[0] // 2
    far = (
        along(ab[:half_a], "y", 1),
        along(aa[half_a:], "y", -1),
        along(bb[:half_b], "x", 1),
        along(ba[half_b:], "x", -1),
    )
    a_low, a_high, b_low, b_high, *rest = together(*far, *beside())
    return [a, ab, aa, a_low, a_high, b, bb, ba, b_low, b_high], rest


def nothing():
    return ()


def locate(outer, inner, rows):
    if outer < 3:
        return outer, inner * rows
    return 3 + inner // 2, (inner % 2) * rows


def locate_out(outer, inner, rows):
    return 2 * outer + inner // 2, (inner % 2) * rows


def add(*terms):
    return functools.reduce(jnp.add, [term.astype(jnp.float32) for term in terms])


def scatter_both(partial):
    rounded = jnp.bfloat16
    sides = [(partial[:8], "y", "x"), (partial[8:], "x", "y")]
    far = []
    for parts, axis, _ in sides:
        far += [along(parts[6], axis, 1), along(parts[7], axis, -1)]
    *far, a3, a4, b3, b4 = together(*far, *(sides[i][0][j] for i in (0, 1) for j in (5, 2)))
    early = []
    for at, (high, low) in enumerate(((a3, a4), (b3, b4))):
        axis = sides[at][1]
        early += [along(high, axis, 1), along(low, axis, -1)]
    sends = []
    for at, (parts, _, _) in enumerate(sides):
        sends += [
            add(parts[4], far[2 * at]).astype(rounded),
            add(parts[3], far[2 * at + 1]).astype(rounded),
        ]
    *early, s0, s1, s2, s3 = together(*early, *sends)
    sends = (s0, s1, s2, s3)
    late = []
    for at, (_, axis, _) in enumerate(sides):
        late += [along(sends[2 * at], axis, 1), along(sends[2 * at + 1], axis, -1)]
    late = together(*late)
    inner = []
    for at, (parts, _, _) in enumerate(sides):
        low = add(parts[0], late[2 * at], early[2 * at + 1]).astype(rounded)
        high = add(parts[1], early[2 * at], late[2 * at + 1]).astype(rounded)
        rows = low.shape[0] // 2
        inner.append((low[:rows], low[rows:], high[:rows], high[rows:]))
    flat = together(*inner[0], *inner[1])
    got = []
    for at, (_, _, axis) in enumerate(sides):
        got += [along(flat[4 * at + 1 + i], axis, step) for i, step in enumerate((-1, 1, 2))]
    got = together(*got)
    return [add(flat[4 * at], *got[3 * at : 3 * at + 3]) for at in range(2)]


def attend_kernel(inner_first, info, q_ref, *refs):
    pieces, out_ref, k_scr, v_scr, sems = refs[:5], refs[5], refs[6], refs[7], refs[8]
    y, x = info[0], info[1]
    chip = y * SIDE + x
    block = 256

    def copies():
        made = []
        for outer in range(SIDE):
            for inner in range(SIDE):
                piece, row = locate(outer, inner, block + TOLD_ROWS if inner_first == "x" else block)
                ry, rx = (OFFSETS[outer], OFFSETS[inner])
                if inner_first == "y":
                    ry, rx = rx, ry
                home = lax.rem(y + ry + SIDE, SIDE) * SIDE + lax.rem(x + rx + SIDE, SIDE)
                home = pl.multiple_of(home * block, block)
                number = outer * SIDE + inner
                source = pieces[piece].at[pl.ds(row, block)]
                made.append(
                    pltpu.make_async_copy(
                        source.at[:, pl.ds(0, HEAD_DIM)],
                        k_scr.at[pl.ds(home, block)],
                        sems.at[0, number],
                    )
                )
                made.append(
                    pltpu.make_async_copy(
                        source.at[:, pl.ds(HEAD_DIM, HEAD_DIM)],
                        v_scr.at[pl.ds(home, block)],
                        sems.at[1, number],
                    )
                )
        return made

    @pl.when(pl.program_id(0) == 0)
    def _():
        for copy in copies():
            copy.start()
        for copy in copies():
            copy.wait()

    scale = HEAD_DIM ** (-0.5) * LOG2E
    keys = 2 * block
    q = jnp.concatenate([q_ref[:, :HEAD_DIM], q_ref[:, HEAD_DIM:]], axis=0)
    rows = q.shape[0]

    def step(at, carry, masked):
        top, total, acc = carry
        begin = pl.multiple_of(at * keys, keys)
        k = k_scr[pl.ds(begin, keys), :]
        v = v_scr[pl.ds(begin, keys), :]
        s = (
            lax.dot_general(q, k, (((1,), (1,)), ((), ())), preferred_element_type=jnp.float32)
            * scale
        )
        if masked:
            row = lax.broadcasted_iota(jnp.int32, s.shape, 0) % block + chip * block
            col = lax.broadcasted_iota(jnp.int32, s.shape, 1) + begin
            s = jnp.where(col <= row, s, -1e30)
        new_top = jnp.maximum(top, jnp.max(s, axis=1, keepdims=True))
        p = jnp.exp2(s - new_top)
        shrink = jnp.exp2(top - new_top)
        total = total * shrink + jnp.sum(p, axis=1, keepdims=True)
        acc = acc * shrink + jnp.dot(
            p.astype(jnp.bfloat16), v, preferred_element_type=jnp.float32
        )
        return new_top, total, acc

    carry = (
        jnp.full((rows, 1), -1e30, jnp.float32),
        jnp.zeros((rows, 1), jnp.float32),
        jnp.zeros((rows, HEAD_DIM), jnp.float32),
    )
    full = chip // 2
    carry = lax.fori_loop(0, full, functools.partial(step, masked=False), carry)
    _, total, acc = step(full, carry, True)
    out = (acc / total).astype(jnp.bfloat16)
    out_ref[:, :HEAD_DIM] = out[:block]
    out_ref[:, HEAD_DIM:] = out[block:]


def attend(info, q, pieces, inner_first):
    tokens, width = q.shape
    at_once = 2 * HEAD_DIM
    spec = pl.BlockSpec((tokens, at_once), lambda i, info: (0, i))
    keys = CHIPS * tokens
    return pl.pallas_call(
        functools.partial(attend_kernel, inner_first),
        out_shape=jax.ShapeDtypeStruct((tokens, width), jnp.bfloat16),
        grid_spec=pltpu.PrefetchScalarGridSpec(
            num_scalar_prefetch=1,
            grid=(width // at_once,),
            in_specs=[spec] + [ANY] * 5,
            out_specs=spec,
            scratch_shapes=[
                pltpu.VMEM((keys, HEAD_DIM), jnp.bfloat16),
                pltpu.VMEM((keys, HEAD_DIM), jnp.bfloat16),
                pltpu.SemaphoreType.DMA((2, CHIPS)),
            ],
        ),
        compiler_params=pltpu.CompilerParams(vmem_limit_bytes=VMEM_LIMIT),
        cost_estimate=pl.CostEstimate(
            flops=4 * tokens * width * keys, bytes_accessed=6 << 20, transcendentals=tokens * width * keys // 128
        ),
    )(info, q, *pieces)


def project_kernel(info, *refs):
    parts, w_ref, keep_ref, send_ref, w_scr, sems = refs[:-5], *refs[-5:]
    c = info[2]
    depth, width = parts[0].shape[1], w_ref.shape[1]
    tokens = keep_ref.shape[0]

    def copy_of(i):
        source = w_ref.at[pl.ds(pl.multiple_of((c * len(parts) + i) * depth, depth), depth)]
        return pltpu.make_async_copy(source, w_scr.at[i], sems.at[i])

    for i in range(len(parts)):
        copy_of(i).start()
    own = pl.ds(pl.multiple_of(c * tokens, tokens), tokens)
    other = pl.ds(pl.multiple_of((1 - c) * tokens, tokens), tokens)
    tile = 512
    for i in range(len(parts)):
        copy_of(i).wait()
    for rows, target in ((other, send_ref), (own, keep_ref)):
        for at in range(0, width, tile):
            product = sum(
                jnp.dot(
                    part[rows, :], w_scr[i, :, at : at + tile], preferred_element_type=jnp.float32
                )
                for i, part in enumerate(parts)
            )
            target[:, at : at + tile] = product.astype(target.dtype)


def project(info, parts, weight):
    width = weight.shape[1]
    tokens = parts[0].shape[0] // CORES
    vmem = pl.BlockSpec(memory_space=pltpu.VMEM)
    depth = parts[0].shape[1]
    return pl.pallas_call(
        project_kernel,
        out_shape=(
            jax.ShapeDtypeStruct((tokens, width), jnp.float32),
            jax.ShapeDtypeStruct((tokens, width), jnp.bfloat16),
        ),
        in_specs=[pl.BlockSpec(memory_space=pltpu.SMEM)] + [vmem] * len(parts) + [ANY],
        out_specs=(vmem, vmem),
        scratch_shapes=[
            pltpu.VMEM((len(parts), depth, width), jnp.bfloat16),
            pltpu.SemaphoreType.DMA((len(parts),)),
        ],
        compiler_params=pltpu.CompilerParams(vmem_limit_bytes=VMEM_LIMIT),
        cost_estimate=pl.CostEstimate(
            flops=4 * tokens * width * depth * len(parts), bytes_accessed=12 << 20, transcendentals=0
        ),
    )(info, *parts, weight)


def expert_kernel(
    row_ref,
    share_ref,
    gate_own,
    up_own,
    down_own,
    gate_sib,
    up_sib,
    down_sib,
    *refs,
):
    pieces, outs = refs[:10], refs[10:26]
    x_scr, h_scr, acc, y_scr, pick_scr, share_scr, in_sems, out_sems = refs[26:]
    expert, chunk = pl.program_id(0), pl.program_id(1)
    pair_count, pair_rows, pair_tokens = pick_scr.shape
    experts = 4
    slots = pair_rows // experts
    block = pair_tokens // 2
    width = x_scr.shape[2]
    half = width // 2

    def moves(hbm, out):
        made = []
        for side in range(2):
            for outer in range(SIDE):
                for inner in range(SIDE):
                    piece, row = (locate_out if out else locate)(outer, inner, block)
                    yi, xi = (outer, inner) if side == 0 else (inner, outer)
                    there = hbm[(8 if out else 5) * side + piece].at[pl.ds(row, block)]
                    here = x_scr.at[
                        yi * 2 + xi // 2, pl.ds((xi % 2) * block, block), pl.ds(side * half, half)
                    ]
                    sems = out_sems if out else in_sems
                    sem = sems.at[side, outer * SIDE + inner]
                    ends = (here, there) if out else (there, here)
                    made.append(pltpu.make_async_copy(*ends, sem))
        return made

    @pl.when((expert == 0) & (chunk == 0))
    def _():
        for copy in moves(pieces, False):
            copy.start()

        @pl.loop(0, pair_count)
        def _(pair):
            slot = lax.broadcasted_iota(jnp.int32, (pair_rows, pair_tokens), 0)
            pick = jnp.zeros((pair_rows, pair_tokens), jnp.float32)
            share = jnp.zeros((pair_rows, pair_tokens), jnp.float32)
            for r in range(TOPK):
                match = row_ref[pair, r : r + 1, :] == slot
                pick = jnp.where(match, 1.0, pick)
                share = jnp.where(match, share_ref[pair, r : r + 1, :], share)
            pick_scr[pair] = pick.astype(jnp.bfloat16)
            share_scr[pair] = jnp.sum(share, axis=1, keepdims=True)

        for copy in moves(pieces, False):
            copy.wait()

        @pl.loop(0, pair_count)
        def _(pair):
            for part in range(2):
                columns = pl.ds(part * half, half)
                rows = jnp.dot(
                    pick_scr[pair], x_scr[pair, :, columns], preferred_element_type=jnp.float32
                ).astype(jnp.bfloat16)
                for e in range(experts):
                    h_scr[e, pl.ds(pl.multiple_of(pair * slots, slots), slots), columns] = rows[
                        e * slots : (e + 1) * slots
                    ]

    def run(gate_ref, up_ref, down_ref):
        rows = h_scr[expert]
        gate = jnp.dot(rows, gate_ref[0], preferred_element_type=jnp.float32)
        up = jnp.dot(rows, up_ref[0], preferred_element_type=jnp.float32)
        hidden = (gate / (1.0 + jnp.exp(-gate)) * up).astype(jnp.bfloat16)
        for part in range(2):
            columns = pl.ds(part * half, half)
            product = jnp.dot(hidden, down_ref[0, :, columns], preferred_element_type=jnp.float32)

            @pl.when(chunk == 0)
            def _():
                acc[:, columns] = product

            @pl.when(chunk > 0)
            def _():
                acc[:, columns] += product

    @pl.when(expert < 2)
    def _():
        run(gate_own, up_own, down_own)

    @pl.when(expert >= 2)
    def _():
        run(gate_sib, up_sib, down_sib)

    last_chunk = chunk == pl.num_programs(1) - 1

    @pl.when(last_chunk)
    def _():
        for pair in range(pair_count):
            rows = acc[pair * slots : (pair + 1) * slots, :] * share_scr[
                pair, pl.ds(pl.multiple_of(expert * slots, slots), slots), :
            ]
            y_scr[pair, pl.ds(pl.multiple_of(expert * slots, slots), slots), :] = rows.astype(
                jnp.bfloat16
            )

    @pl.when(last_chunk & (expert == experts - 1))
    def _():
        @pl.loop(0, pair_count)
        def _(pair):
            for part in range(2):
                columns = pl.ds(part * half, half)
                x_scr[pair, :, columns] = lax.dot_general(
                    pick_scr[pair],
                    y_scr[pair, :, columns],
                    (((0,), (0,)), ((), ())),
                    preferred_element_type=jnp.float32,
                ).astype(jnp.bfloat16)

        for copy in moves(outs, True):
            copy.start()
        for copy in moves(outs, True):
            copy.wait()


def run_experts(row, share, own, sib, pieces):
    pair_count, _, pair_tokens = row.shape
    pair_rows = 4 * 2 * 3 * (pair_tokens // 2) * TOPK // (2 * 4 * CHIPS)
    width = own[0].shape[1]
    hidden = own[0].shape[2]
    chunks = 3
    tile = hidden // chunks
    experts = 4
    slots = pair_rows // experts
    whole = pl.BlockSpec(memory_space=pltpu.VMEM)

    def own_in(e, f):
        return (jnp.minimum(e, 1), 0, jnp.where(e < 2, f, chunks - 1))

    def own_out(e, f):
        return (jnp.minimum(e, 1), jnp.where(e < 2, f, chunks - 1), 0)

    def sib_in(e, f):
        return (jnp.maximum(e - 2, 0), 0, jnp.where(e < 2, 0, f))

    def sib_out(e, f):
        return (jnp.maximum(e - 2, 0), jnp.where(e < 2, 0, f), 0)

    rows = experts * pair_count * slots
    return pl.pallas_call(
        expert_kernel,
        grid=(experts, chunks),
        out_shape=[jax.ShapeDtypeStruct(pieces[3].shape, jnp.bfloat16)] * 16,
        in_specs=[
            whole,
            whole,
            pl.BlockSpec((1, width, tile), own_in),
            pl.BlockSpec((1, width, tile), own_in),
            pl.BlockSpec((1, tile, width), own_out),
            pl.BlockSpec((1, width, tile), sib_in),
            pl.BlockSpec((1, width, tile), sib_in),
            pl.BlockSpec((1, tile, width), sib_out),
        ]
        + [ANY] * 10,
        out_specs=[ANY] * 16,
        scratch_shapes=[
            pltpu.VMEM((pair_count, pair_tokens, width), jnp.bfloat16),
            pltpu.VMEM((experts, pair_count * slots, width), jnp.bfloat16),
            pltpu.VMEM((pair_count * slots, width), jnp.float32),
            pltpu.VMEM((pair_count, pair_rows, width), jnp.bfloat16),
            pltpu.VMEM((pair_count, pair_rows, pair_tokens), jnp.bfloat16),
            pltpu.VMEM((pair_count, pair_rows, 1), jnp.float32),
            pltpu.SemaphoreType.DMA((2, CHIPS)),
            pltpu.SemaphoreType.DMA((2, CHIPS)),
        ],
        compiler_params=pltpu.CompilerParams(vmem_limit_bytes=VMEM_LIMIT),
        cost_estimate=pl.CostEstimate(
            flops=6 * rows * width * hidden, bytes_accessed=56 << 20, transcendentals=rows * hidden
        ),
    )(row, share, *own, *sib, *pieces)


def told_routes(routes, route_gates, experts_all):
    tokens = routes.shape[0]
    share = route_gates / jnp.sum(route_gates, axis=1, keepdims=True)
    named = (routes[:, :, None] == jnp.arange(experts_all, dtype=jnp.int32)).astype(jnp.float32)
    hits = jnp.sum(named, axis=1)
    order = jnp.arange(tokens)
    earlier = (order[None, :] < order[:, None]).astype(jnp.bfloat16)
    rank = jnp.dot(earlier, hits.astype(jnp.bfloat16), preferred_element_type=jnp.float32)
    rank = jnp.sum(named * rank[:, None, :], axis=2)
    high = share.astype(jnp.bfloat16)
    left = share - high.astype(jnp.float32)
    mid = left.astype(jnp.bfloat16)
    low = (left - mid.astype(jnp.float32)).astype(jnp.bfloat16)
    first = jnp.concatenate([routes.astype(jnp.bfloat16).T, high.T, low.T], axis=0)
    second = jnp.concatenate([rank.astype(jnp.bfloat16).T, mid.T, jnp.zeros_like(low.T)], axis=0)
    told = jnp.concatenate([first, second], axis=1)
    return jnp.pad(told, ((0, TOLD_ROWS - 3 * TOPK), (0, 0)))


def route_tables(told, y, x, c):
    tokens = told.shape[2] // 2
    capacity = 3 * tokens * TOPK // (2 * 4 * CHIPS)
    expert = told[:, :TOPK, :tokens].astype(jnp.int32)
    rank = told[:, :TOPK, tokens:].astype(jnp.int32)
    share = (
        told[:, TOPK : 2 * TOPK, :tokens].astype(jnp.float32)
        + told[:, TOPK : 2 * TOPK, tokens:].astype(jnp.float32)
        + told[:, 2 * TOPK : 3 * TOPK, :tokens].astype(jnp.float32)
    )
    local = expert - (y * SIDE + x) * 4
    here = (local >= 0) & (local < 4)
    local = (local + 4 - 2 * c) % 4
    second = (jnp.arange(CHIPS, dtype=jnp.int32) % 2)[:, None, None]
    row = jnp.where(here, (local * 2 + second) * capacity + rank, -1)

    def paired(array):
        array = array.reshape(CHIPS // 2, 2, TOPK, tokens)
        return jnp.concatenate([array[:, 0], array[:, 1]], axis=2)

    return paired(row), paired(share)


def in_order(c, mine, theirs):
    return jnp.where(
        c == 0, jnp.concatenate([mine, theirs], axis=0), jnp.concatenate([theirs, mine], axis=0)
    )


def body(
    queries,
    key_vectors,
    value_vectors,
    residual,
    out_weight,
    norm_gain,
    routes,
    route_gates,
    w_gate,
    w_up,
    w_down,
):
    me = lax.axis_index("seq")
    c = me % CORES
    x = me // CORES % SIDE
    y = me // (CORES * SIDE)
    info = jnp.stack([y, x, c]).astype(jnp.int32)
    tokens, width = residual.shape
    experts_all = w_gate.shape[0] * lax.axis_size("seq")

    kv_half = key_vectors.shape[1] // 2
    q_half = queries.shape[1] // 2

    def half_of(array, which, size):
        return lax.dynamic_slice_in_dim(array, which * size, size, axis=1)

    def kv_of(which):
        k, v = (half_of(a, which, kv_half) for a in (key_vectors, value_vectors))
        d = HEAD_DIM
        return jnp.concatenate([k[:, :d], v[:, :d], k[:, d:], v[:, d:]], axis=1)

    kv_send, q_send = together(kv_of(1 - c), half_of(queries, 1 - c, q_half))
    kv = in_order(c, kv_of(c), to_sibling(kv_send))
    q_got = to_sibling(q_send)
    told = told_routes(routes, route_gates, experts_all)
    kv_a = jnp.concatenate([kv[:, : 2 * HEAD_DIM], told], axis=0)
    kv_b = kv[:, 2 * HEAD_DIM :]

    weight = lax.all_gather(out_weight, "seq", axis=0, tiled=True)
    own = (w_gate, w_up, w_down)

    kv_lines = near(kv_a, kv_b)
    kv_wide = wide(*kv_lines, nothing)
    kv_pieces, _ = wide_far(*kv_lines, kv_wide, nothing)
    q = in_order(c, half_of(queries, c, q_half), q_got)
    *sends, q = together(*own, q, kv_pieces[0])[:4]
    sib = [to_sibling(w) for w in sends]
    att_0 = attend(info, q[:, : q_half // 2], kv_pieces[:5], "x")
    att_1 = attend(info, q[:, q_half // 2 :], kv_pieces[5:], "y")

    keep, send = project(info, (att_0, att_1), weight)
    attn_sum = keep + to_sibling(send).astype(jnp.float32)
    stream = (residual.astype(jnp.float32) + attn_sum).astype(jnp.bfloat16)
    stream_f = stream.astype(jnp.float32)
    normed = (
        stream_f
        * lax.rsqrt(jnp.mean(stream_f * stream_f, axis=1, keepdims=True) + 1e-06)
        * norm_gain
    ).astype(jnp.bfloat16)

    told_rows = 2 * tokens + TOLD_ROWS
    told = []
    for outer in range(SIDE):
        for inner in range(SIDE):
            piece, first_row = locate(outer, inner, told_rows)
            first_row += 2 * tokens
            told.append(kv_pieces[piece][first_row : first_row + TOLD_ROWS])
    row, share = route_tables(jnp.stack(told), y, x, c)

    x_lines = near(normed[:, : width // 2], normed[:, width // 2 :])
    x_wide = wide(*x_lines, nothing)
    x_pieces, _ = wide_far(*x_lines, x_wide, nothing)
    partial = run_experts(row, share, own, sib, x_pieces)
    expert_sum = jnp.concatenate(scatter_both(partial), axis=1)
    layer_out = (stream_f + expert_sum).astype(jnp.bfloat16)
    return (stream, layer_out)


def solution(mesh):
    in_specs = (
        P(("dp", "seq"), None),
        P(("dp", "seq"), None),
        P(("dp", "seq"), None),
        P(("dp", "seq"), None),
        P("seq", None),
        P(),
        P(("dp", "seq"), None),
        P(("dp", "seq"), None),
        P("seq", None, None),
        P("seq", None, None),
        P("seq", None, None),
    )
    out_specs = (P(("dp", "seq"), None), P(("dp", "seq"), None))
    return jax.shard_map(body, mesh=mesh, in_specs=in_specs, out_specs=out_specs, check_vma=False)
```

```python
import functools

import jax
import jax.numpy as jnp
from jax import lax
from jax.experimental import pallas as pl
from jax.experimental.pallas import tpu as pltpu
from jax.sharding import PartitionSpec as P

HEADS = 32
KV_HEADS = 4
HEAD_DIM = 128
TOPK = 8
SIDE = 4
CHIPS = SIDE * SIDE
CORES = 2
OFFSETS = (0, -1, 1, 2)
TOLD_ROWS = 16
LOG2E = 1.4426950408889634
ANY = pl.BlockSpec(memory_space=pl.ANY)
VMEM_LIMIT = 60 * 1024 * 1024


def ring_pairs(stage, step):
    pairs = []
    for y in range(SIDE):
        for x in range(SIDE):
            for c in range(CORES):
                dy, dx = (step, 0) if stage != c else (0, step)
                source = (y * SIDE + x) * CORES + c
                target = ((y + dy) % SIDE * SIDE + (x + dx) % SIDE) * CORES + c
                pairs.append((source, target))
    return pairs


def along(value, stage, step):
    return lax.ppermute(value, "seq", ring_pairs(stage, step))


def to_sibling(value):
    devices = CHIPS * CORES
    return lax.ppermute(value, "seq", [(d, d ^ 1) for d in range(devices)])


def together(*values):
    return lax.optimization_barrier(values)


def gather_grid(block):
    line = jnp.concatenate([block, *(along(block, 0, step) for step in (1, -1, 2))], axis=0)
    before, after = along(line, 1, 1), along(line, 1, -1)
    half = line.shape[0] // 2
    far = along(before[:half], 1, 1), along(after[half:], 1, -1)
    return [line, before, after, *far]


def locate(outer, inner, rows):
    if outer < 3:
        return outer, inner * rows
    return 3 + inner // 2, (inner % 2) * rows


def add(*terms):
    return functools.reduce(jnp.add, [term.astype(jnp.float32) for term in terms])


def scatter_grid(halves):
    rounded = jnp.bfloat16
    own_low, own_high, before_low, before_high, after_low, after_high, far_low, far_high = halves
    got_low, got_high = along(far_low, 1, 1), along(far_high, 1, -1)
    early_high, early_low = along(after_high, 1, 1), along(before_low, 1, -1)
    late_low = along(add(after_low, got_low).astype(rounded), 1, 1)
    late_high = along(add(before_high, got_high).astype(rounded), 1, -1)
    low = add(own_low, late_low, early_low).astype(rounded)
    high = add(own_high, early_high, late_high).astype(rounded)
    rows = low.shape[0] // 2
    own, before, after, far = low[:rows], low[rows:], high[:rows], high[rows:]
    return add(own, along(after, 0, 1), along(before, 0, -1), along(far, 0, 2))


def norm_kernel(keep_ref, got_ref, residual_ref, gain_ref, stream_ref, normed_ref):
    attn_sum = keep_ref[...] + got_ref[...].astype(jnp.float32)
    stream = (residual_ref[...].astype(jnp.float32) + attn_sum).astype(jnp.bfloat16)
    stream_ref[...] = stream
    stream = stream.astype(jnp.float32)
    mean = jnp.mean(stream * stream, axis=1, keepdims=True)
    normed_ref[...] = (stream * lax.rsqrt(mean + 1e-06) * gain_ref[...]).astype(jnp.bfloat16)


def norm(keep, got, residual, gain):
    tokens, width = residual.shape
    whole = jax.ShapeDtypeStruct((tokens, width), jnp.bfloat16)
    return pl.pallas_call(
        norm_kernel,
        out_shape=(whole, whole),
        cost_estimate=pl.CostEstimate(
            flops=8 * tokens * width, bytes_accessed=14 * tokens * width, transcendentals=tokens
        ),
        name="norm",
    )(keep, got, residual, gain[None, :])


def attend_kernel(info, q_ref, *refs):
    pieces, out_ref, k_scr, v_scr, turned, sems = refs[:5], *refs[5:]
    y, x, c = info[0], info[1], info[2]
    chip = y * SIDE + x
    block = 256
    group = pl.program_id(0) // 2

    def copies(side):
        made = []
        for outer in range(SIDE):
            for inner in range(SIDE):
                piece, row = locate(outer, inner, block + TOLD_ROWS)
                ry = jnp.where(c == 0, OFFSETS[outer], OFFSETS[inner])
                rx = jnp.where(c == 0, OFFSETS[inner], OFFSETS[outer])
                home = lax.rem(y + ry + SIDE, SIDE) * SIDE + lax.rem(x + rx + SIDE, SIDE)
                home = pl.ds(pl.multiple_of(home * block, block), block)
                source = pieces[piece].at[pl.ds(row, block)]
                for which, scr in enumerate((k_scr, v_scr)):
                    columns = pl.ds((2 * side + which) * HEAD_DIM, HEAD_DIM)
                    sem = sems.at[side, which, outer * SIDE + inner]
                    made.append(
                        pltpu.make_async_copy(source.at[:, columns], scr.at[side, home], sem)
                    )
        return made

    def arrive(side):
        for copy in copies(side):
            copy.wait()

        @pl.loop(0, CHIPS)
        def _(at):
            columns = pl.ds(pl.multiple_of(at * block, block), block)
            turned[:, columns] = v_scr[side, columns, :].astype(jnp.float32).T.astype(jnp.bfloat16)

    @pl.when(pl.program_id(0) == 0)
    def _():
        for side in range(2):
            for copy in copies(side):
                copy.start()
        arrive(0)

    @pl.when(pl.program_id(0) == 2)
    def _():
        arrive(1)

    scale = HEAD_DIM ** (-0.5) * LOG2E
    keys = 4 * block
    heads = q_ref.shape[1] // HEAD_DIM
    q = jnp.concatenate(
        [q_ref[:, h * HEAD_DIM : (h + 1) * HEAD_DIM] for h in range(heads)], axis=0
    )
    rows = q.shape[0]

    def step(at, carry, masked):
        top, total, acc = carry
        begin = pl.multiple_of(at * keys, keys)
        s = (
            lax.dot_general(
                k_scr[group, pl.ds(begin, keys), :],
                q,
                (((1,), (1,)), ((), ())),
                preferred_element_type=jnp.float32,
            )
            * scale
        )
        if masked:
            key = lax.broadcasted_iota(jnp.int32, s.shape, 0) + begin
            query = lax.broadcasted_iota(jnp.int32, s.shape, 1) % block + chip * block
            s = jnp.where(key <= query, s, -1e30)
        new_top = jnp.maximum(top, jnp.max(s, axis=0, keepdims=True))
        p = jnp.exp2(s - new_top)
        shrink = jnp.exp2(top - new_top)
        total = total * shrink + jnp.sum(p, axis=0, keepdims=True)
        acc = acc * shrink + jnp.dot(
            turned[:, pl.ds(begin, keys)],
            p.astype(jnp.bfloat16),
            preferred_element_type=jnp.float32,
        )
        return new_top, total, acc

    carry = (
        jnp.full((1, rows), -1e30, jnp.float32),
        jnp.zeros((1, rows), jnp.float32),
        jnp.zeros((HEAD_DIM, rows), jnp.float32),
    )
    full = chip * block // keys
    carry = lax.fori_loop(0, full, functools.partial(step, masked=False), carry)
    _, total, acc = step(full, carry, True)
    out = (acc / total).T.astype(jnp.bfloat16)
    for h in range(heads):
        out_ref[:, h * HEAD_DIM : (h + 1) * HEAD_DIM] = out[h * block : (h + 1) * block]


def attend(info, q, pieces):
    tokens, width = q.shape
    at_once = width // 4
    spec = pl.BlockSpec((tokens, at_once), lambda i, info: (0, i))
    keys = CHIPS * tokens
    return pl.pallas_call(
        attend_kernel,
        out_shape=jax.ShapeDtypeStruct((tokens, width), jnp.bfloat16),
        grid_spec=pltpu.PrefetchScalarGridSpec(
            num_scalar_prefetch=1,
            grid=(width // at_once,),
            in_specs=[spec] + [ANY] * 5,
            out_specs=spec,
            scratch_shapes=[
                pltpu.VMEM((2, keys, HEAD_DIM), jnp.bfloat16),
                pltpu.VMEM((2, keys, HEAD_DIM), jnp.bfloat16),
                pltpu.VMEM((HEAD_DIM, keys), jnp.bfloat16),
                pltpu.SemaphoreType.DMA((2, 2, CHIPS)),
            ],
        ),
        compiler_params=pltpu.CompilerParams(vmem_limit_bytes=VMEM_LIMIT),
        cost_estimate=pl.CostEstimate(
            flops=4 * tokens * width * keys,
            bytes_accessed=6 << 20,
            transcendentals=tokens * width * keys // HEAD_DIM,
        ),
    )(info, q, *pieces)


def project_kernel(info, *refs):
    parts, w_ref, keep_ref, send_ref, w_scr, sems = refs[:-5], *refs[-5:]
    c = info[2]
    depth, width = parts[0].shape[1], w_ref.shape[1]
    tokens = keep_ref.shape[0]

    own = pl.ds(pl.multiple_of(c * tokens, tokens), tokens)
    other = pl.ds(pl.multiple_of((1 - c) * tokens, tokens), tokens)
    tiles = w_scr.shape[0]
    tile = width // tiles
    part = parts[0]

    def copy_of(i):
        source = w_ref.at[pl.ds(pl.multiple_of(c * depth, depth), depth), pl.ds(i * tile, tile)]
        return pltpu.make_async_copy(source, w_scr.at[i], sems.at[i])

    for i in range(tiles):
        copy_of(i).start()
    for i in range(tiles):
        copy_of(i).wait()
        for rows, target in ((other, send_ref), (own, keep_ref)):
            product = jnp.dot(part[rows, :], w_scr[i], preferred_element_type=jnp.float32)
            target[:, i * tile : (i + 1) * tile] = product.astype(target.dtype)


def project(info, parts, weight):
    width = weight.shape[1]
    tokens = parts[0].shape[0] // CORES
    vmem = pl.BlockSpec(memory_space=pltpu.VMEM)
    depth = parts[0].shape[1]
    return pl.pallas_call(
        project_kernel,
        out_shape=(
            jax.ShapeDtypeStruct((tokens, width), jnp.float32),
            jax.ShapeDtypeStruct((tokens, width), jnp.bfloat16),
        ),
        in_specs=[pl.BlockSpec(memory_space=pltpu.SMEM)] + [vmem] * len(parts) + [ANY],
        out_specs=(vmem, vmem),
        scratch_shapes=[
            pltpu.VMEM((8, depth, width // 8), jnp.bfloat16),
            pltpu.SemaphoreType.DMA((8,)),
        ],
        compiler_params=pltpu.CompilerParams(vmem_limit_bytes=VMEM_LIMIT),
        cost_estimate=pl.CostEstimate(
            flops=4 * tokens * width * depth * len(parts), bytes_accessed=12 << 20, transcendentals=0
        ),
    )(info, *parts, weight)


def expert_kernel(info, *refs):
    told, weights, pieces, outs = refs[:5], (refs[5:8], refs[8:11]), refs[11:16], refs[16:24]
    told_scr, pick_scr, put_scr, share_scr, x_scr, h_scr, hid_scr, y_scr = refs[24:32]
    gate_scr, up_scr, down_scr, told_sems, in_sems, out_sems, w_sems = refs[32:]
    pair_count, pair_rows, pair_tokens = pick_scr.shape
    experts = 4
    slots = pair_rows // experts
    block = pair_tokens // 2
    width = x_scr.shape[2]
    half = width // 2
    buffers = (gate_scr, up_scr, down_scr)

    def weight_copy(e, which):
        source = weights[e // 2][which].at[e % 2]
        return pltpu.make_async_copy(
            source, buffers[which].at[e % 2], w_sems.at[which, e % 2]
        )

    def load(pair):
        piece, row = locate(pair // 2, pair % 2 * 2, block)
        source = pieces[piece].at[pl.ds(row, pair_tokens)]
        return pltpu.make_async_copy(source, x_scr.at[pair], in_sems.at[pair])

    def store(pair):
        return pltpu.make_async_copy(x_scr.at[pair], outs[pair], out_sems.at[pair])

    told_copies = []
    for yi in range(SIDE):
        for xi in range(SIDE):
            piece, row = locate(yi, xi, CORES * block + TOLD_ROWS)
            number = yi * SIDE + xi
            told_copies.append(
                pltpu.make_async_copy(
                    told[piece].at[pl.ds(row + CORES * block, TOLD_ROWS)],
                    told_scr.at[number],
                    told_sems.at[number],
                )
            )
    for copy in told_copies:
        copy.start()
    for pair in range(pair_count):
        load(pair).start()
    for e in range(2):
        for which in range(3):
            weight_copy(e, which).start()
    for copy in told_copies:
        copy.wait()

    first_expert = (info[0] * SIDE + info[1]) * experts
    own_first = 2 * info[2]

    def routes_of(number, at):
        rows = told_scr[number].astype(jnp.float32)
        expert, rank, high, mid = (rows[:TOPK, i * block : (i + 1) * block] for i in range(4))
        share = high + mid + rows[TOPK:, :block]
        local = expert.astype(jnp.int32) - first_expert
        here = (local >= 0) & (local < experts)
        local = local - own_first
        local = jnp.where(local < 0, local + experts, local)
        row = local * slots + at * (slots // 2) + rank.astype(jnp.int32)
        return jnp.where(here, row, -1), share

    @pl.loop(0, pair_count)
    def _(pair):
        row, share = zip(*(routes_of(2 * pair + at, at) for at in range(2)))
        row, share = jnp.concatenate(row, axis=1), jnp.concatenate(share, axis=1)
        slot = lax.broadcasted_iota(jnp.int32, (pair_rows, pair_tokens), 0)
        pick = jnp.zeros(slot.shape, jnp.float32)
        shares = jnp.zeros(slot.shape, jnp.float32)
        for r in range(TOPK):
            match = row[r : r + 1, :] == slot
            pick = jnp.where(match, 1.0, pick)
            shares = jnp.where(match, share[r : r + 1, :], shares)
        pick_scr[pair] = pick.astype(jnp.bfloat16)
        put_scr[pair] = pick.T.astype(jnp.bfloat16)
        share_scr[pair] = jnp.sum(shares, axis=1, keepdims=True)

    for pair in range(pair_count):
        load(pair).wait()
        for part in range(2):
            columns = pl.ds(part * half, half)
            rows = jnp.dot(
                pick_scr[pair], x_scr[pair, :, columns], preferred_element_type=jnp.float32
            ).astype(jnp.bfloat16)
            for e in range(experts):
                h_scr[e, pl.ds(pair * slots, slots), columns] = rows[e * slots : (e + 1) * slots]

    tile, wide_tile = 256, 512
    for e in range(experts):
        at = e % 2
        weight_copy(e, 0).wait()
        weight_copy(e, 1).wait()
        for begin in range(0, hid_scr.shape[1], tile):
            columns = pl.ds(begin, tile)
            gate = jnp.dot(h_scr[e], gate_scr[at, :, columns], preferred_element_type=jnp.float32)
            up = jnp.dot(h_scr[e], up_scr[at, :, columns], preferred_element_type=jnp.float32)
            hid_scr[:, columns] = (gate / (1.0 + jnp.exp(-gate)) * up).astype(jnp.bfloat16)
        if e + 2 < experts:
            weight_copy(e + 2, 0).start()
            weight_copy(e + 2, 1).start()
        weight_copy(e, 2).wait()
        for begin in range(0, width, wide_tile):
            columns = pl.ds(begin, wide_tile)
            rows = jnp.dot(hid_scr[...], down_scr[at, :, columns], preferred_element_type=jnp.float32)
            for pair in range(pair_count):
                y_scr[pair, pl.ds(e * slots, slots), columns] = (
                    rows[pair * slots : (pair + 1) * slots]
                    * share_scr[pair, pl.ds(e * slots, slots), :]
                ).astype(jnp.bfloat16)
        if e + 2 < experts:
            weight_copy(e + 2, 2).start()

    for pair in reversed(range(pair_count)):
        for part in range(2):
            columns = pl.ds(part * half, half)
            x_scr[pair, :, columns] = jnp.dot(
                put_scr[pair], y_scr[pair, :, columns], preferred_element_type=jnp.float32
            ).astype(jnp.bfloat16)
        store(pair).start()
    for pair in range(pair_count):
        store(pair).wait()


def run_experts(info, told, own, sib, pieces):
    width, hidden = own[0].shape[1:]
    experts = 4
    pair_count = CHIPS // 2
    pair_tokens = pieces[0].shape[0] // SIDE * 2
    slots = 3 * pair_tokens * TOPK // (2 * experts * CHIPS)
    pair_rows = experts * slots
    rows = pair_count * slots
    return pl.pallas_call(
        expert_kernel,
        out_shape=[jax.ShapeDtypeStruct(pieces[3].shape, jnp.bfloat16)] * pair_count,
        in_specs=[pl.BlockSpec(memory_space=pltpu.SMEM)] + [ANY] * 16,
        out_specs=[ANY] * pair_count,
        scratch_shapes=[
            pltpu.VMEM((CHIPS, TOLD_ROWS, told[0].shape[1]), jnp.bfloat16),
            pltpu.VMEM((pair_count, pair_rows, pair_tokens), jnp.bfloat16),
            pltpu.VMEM((pair_count, pair_tokens, pair_rows), jnp.bfloat16),
            pltpu.VMEM((pair_count, pair_rows, 1), jnp.float32),
            pltpu.VMEM((pair_count, pair_tokens, width), jnp.bfloat16),
            pltpu.VMEM((experts, rows, width), jnp.bfloat16),
            pltpu.VMEM((rows, hidden), jnp.bfloat16),
            pltpu.VMEM((pair_count, pair_rows, width), jnp.bfloat16),
            pltpu.VMEM((2, width, hidden), jnp.bfloat16),
            pltpu.VMEM((2, width, hidden), jnp.bfloat16),
            pltpu.VMEM((2, hidden, width), jnp.bfloat16),
            pltpu.SemaphoreType.DMA((CHIPS,)),
            pltpu.SemaphoreType.DMA((pair_count,)),
            pltpu.SemaphoreType.DMA((pair_count,)),
            pltpu.SemaphoreType.DMA((3, 2)),
        ],
        compiler_params=pltpu.CompilerParams(vmem_limit_bytes=VMEM_LIMIT),
        cost_estimate=pl.CostEstimate(
            flops=6 * experts * rows * width * hidden,
            bytes_accessed=56 << 20,
            transcendentals=experts * rows * hidden,
        ),
    )(info, *told, *own, *sib, *pieces)


def told_routes(routes, route_gates, experts_all):
    tokens = routes.shape[0]
    share = route_gates / jnp.sum(route_gates, axis=1, keepdims=True)
    named = (routes[:, :, None] == jnp.arange(experts_all, dtype=jnp.int32)).astype(jnp.float32)
    hits = jnp.sum(named, axis=1)
    order = jnp.arange(tokens)
    earlier = (order[None, :] < order[:, None]).astype(jnp.bfloat16)
    rank = jnp.dot(earlier, hits.astype(jnp.bfloat16), preferred_element_type=jnp.float32)
    rank = jnp.sum(named * rank[:, None, :], axis=2)
    high = share.astype(jnp.bfloat16)
    left = share - high.astype(jnp.float32)
    mid = left.astype(jnp.bfloat16)
    low = (left - mid.astype(jnp.float32)).astype(jnp.bfloat16)
    first = jnp.concatenate([routes.astype(jnp.bfloat16).T, rank.astype(jnp.bfloat16).T, high.T, mid.T], axis=1)
    return jnp.concatenate([first, jnp.pad(low.T, ((0, 0), (0, 3 * tokens)))], axis=0)


def in_order(c, mine, theirs):
    return jnp.where(
        c == 0, jnp.concatenate([mine, theirs], axis=0), jnp.concatenate([theirs, mine], axis=0)
    )


def body(
    queries,
    key_vectors,
    value_vectors,
    residual,
    out_weight,
    norm_gain,
    routes,
    route_gates,
    w_gate,
    w_up,
    w_down,
):
    me = lax.axis_index("seq")
    c = me % CORES
    x = me // CORES % SIDE
    y = me // (CORES * SIDE)
    info = jnp.stack([y, x, c]).astype(jnp.int32)
    tokens, width = residual.shape
    experts_all = w_gate.shape[0] * lax.axis_size("seq")

    kv_half = key_vectors.shape[1] // 2
    q_half = queries.shape[1] // 2

    def half_of(array, which, size):
        return lax.dynamic_slice_in_dim(array, which * size, size, axis=1)

    def kv_of(which):
        k, v = (half_of(a, which, kv_half) for a in (key_vectors, value_vectors))
        d = HEAD_DIM
        return jnp.concatenate([k[:, :d], v[:, :d], k[:, d:], v[:, d:]], axis=1)

    kv_send, q_send = together(kv_of(1 - c), half_of(queries, 1 - c, q_half))
    kv = in_order(c, kv_of(c), to_sibling(kv_send))
    q_got = to_sibling(q_send)
    told = told_routes(routes, route_gates, experts_all)
    kv = jnp.concatenate([kv, told], axis=0)

    weight = lax.all_gather(out_weight, "seq", axis=0, tiled=True)
    own = (w_gate, w_up, w_down)

    kv_pieces = gather_grid(kv)
    q = in_order(c, half_of(queries, c, q_half), q_got)
    *sends, q = together(*own, q, kv_pieces[0])[:4]
    sib = [to_sibling(w) for w in sends]
    attended = attend(info, q, kv_pieces)
    keep, send = project(info, (attended,), weight)
    stream, normed = norm(keep, to_sibling(send), residual, norm_gain)
    partial = run_experts(info, kv_pieces, own, sib, gather_grid(normed))
    expert_sum = scatter_grid(partial)
    layer_out = (stream.astype(jnp.float32) + expert_sum).astype(jnp.bfloat16)
    return (stream, layer_out)


def solution(mesh):
    in_specs = (
        P(("dp", "seq"), None),
        P(("dp", "seq"), None),
        P(("dp", "seq"), None),
        P(("dp", "seq"), None),
        P("seq", None),
        P(),
        P(("dp", "seq"), None),
        P(("dp", "seq"), None),
        P("seq", None, None),
        P("seq", None, None),
        P("seq", None, None),
    )
    out_specs = (P(("dp", "seq"), None), P(("dp", "seq"), None))
    return jax.shard_map(body, mesh=mesh, in_specs=in_specs, out_specs=out_specs, check_vma=False)
```

```python
import functools

import jax
import jax.numpy as jnp
from jax import lax
from jax.experimental import pallas as pl
from jax.experimental.pallas import tpu as pltpu
from jax.sharding import PartitionSpec as P

HEADS = 32
KV_HEADS = 4
HEAD_DIM = 128
TOPK = 8
SIDE = 4
CHIPS = SIDE * SIDE
CORES = 2
OFFSETS = (0, -1, 1, 2)
TOLD_ROWS = 16
LOG2E = 1.4426950408889634
ANY = pl.BlockSpec(memory_space=pl.ANY)
VMEM_LIMIT = 60 * 1024 * 1024


def ring_pairs(stage, step):
    pairs = []
    for y in range(SIDE):
        for x in range(SIDE):
            for c in range(CORES):
                dy, dx = (step, 0) if stage != c else (0, step)
                source = (y * SIDE + x) * CORES + c
                target = ((y + dy) % SIDE * SIDE + (x + dx) % SIDE) * CORES + c
                pairs.append((source, target))
    return pairs


def along(value, stage, step):
    return lax.ppermute(value, "seq", ring_pairs(stage, step))


def to_sibling(value):
    devices = CHIPS * CORES
    return lax.ppermute(value, "seq", [(d, d ^ 1) for d in range(devices)])


def together(*values):
    return lax.optimization_barrier(values)


def rearrange(sources, plan, name, behind=()):
    width = sources[0].shape[1]

    def kernel(*refs):
        ins, outs = refs[: len(sources)], refs[len(sources) + len(behind) :]
        for out, parts in zip(outs, plan):
            at = 0
            for source, begin, rows in parts:
                out[at : at + rows, :] = ins[source][begin : begin + rows, :]
                at += rows

    rows_out = [sum(rows for _, _, rows in parts) for parts in plan]
    return pl.pallas_call(
        kernel,
        out_shape=[jax.ShapeDtypeStruct((rows, width), sources[0].dtype) for rows in rows_out],
        in_specs=[pl.BlockSpec(memory_space=pltpu.VMEM)] * len(sources) + [ANY] * len(behind),
        compiler_params=pltpu.CompilerParams(vmem_limit_bytes=24 * 1024 * 1024),
        cost_estimate=pl.CostEstimate(
            flops=0, bytes_accessed=4 * width * sum(rows_out), transcendentals=0
        ),
        name=name,
    )(*sources, *behind)


def gather_near(block):
    rows = block.shape[0]
    got = [along(block, 0, step) for step in (1, -1, 2)]
    return rearrange([block, *got], [[(i, 0, rows) for i in range(SIDE)]], "line")[0]


def gather_wide(line):
    return along(line, 1, 1), along(line, 1, -1)


def gather_far(before, after, behind=()):
    half = before.shape[0] // 2
    low, high = rearrange([before, after], [[(0, 0, half)], [(1, half, half)]], "halves", behind)
    return low, (along(low, 1, 1), along(high, 1, -1))


def locate(outer, inner, rows):
    if outer < 3:
        return outer, inner * rows
    return 3 + inner // 2, (inner % 2) * rows


def add(*terms):
    return functools.reduce(jnp.add, [term.astype(jnp.float32) for term in terms])


def add_kernel(a_ref, b_ref, c_ref, d_ref, low_ref, high_ref):
    low_ref[...] = add(a_ref[...], b_ref[...]).astype(low_ref.dtype)
    high_ref[...] = add(c_ref[...], d_ref[...]).astype(high_ref.dtype)


def add_pairs(*terms):
    shape = jax.ShapeDtypeStruct(terms[0].shape, terms[0].dtype)
    return pl.pallas_call(
        add_kernel,
        out_shape=(shape, shape),
        compiler_params=pltpu.CompilerParams(vmem_limit_bytes=24 * 1024 * 1024),
        cost_estimate=pl.CostEstimate(
            flops=2 * terms[0].size, bytes_accessed=12 * terms[0].size, transcendentals=0
        ),
        name="add_pairs",
    )(*terms)


def scatter_grid(halves):
    rounded = jnp.bfloat16
    own_low, own_high, before_low, before_high, after_low, after_high, far_low, far_high = halves
    early_high, early_low = along(after_high, 1, 1), along(before_low, 1, -1)
    whole = [[(i, 0, far_low.shape[0])] for i in range(2)]
    far_low, far_high = rearrange([far_low, far_high], whole, "far", (early_high, early_low))
    got_low, got_high = along(far_low, 1, 1), along(far_high, 1, -1)
    low, high = add_pairs(after_low, got_low, before_high, got_high)
    late_low, late_high = along(low, 1, 1), along(high, 1, -1)
    low = add(own_low, late_low, early_low).astype(rounded)
    high = add(own_high, early_high, late_high).astype(rounded)
    rows = low.shape[0] // 2
    own, before, after, far = low[:rows], low[rows:], high[:rows], high[rows:]
    return add(own, along(after, 0, 1), along(before, 0, -1), along(far, 0, 2))


def norm_kernel(keep_ref, got_ref, residual_ref, gain_ref, stream_ref, normed_ref):
    attn_sum = keep_ref[...] + got_ref[...].astype(jnp.float32)
    stream = (residual_ref[...].astype(jnp.float32) + attn_sum).astype(jnp.bfloat16)
    stream_ref[...] = stream
    stream = stream.astype(jnp.float32)
    mean = jnp.mean(stream * stream, axis=1, keepdims=True)
    normed_ref[...] = (stream * lax.rsqrt(mean + 1e-06) * gain_ref[...]).astype(jnp.bfloat16)


def norm(keep, got, residual, gain):
    tokens, width = residual.shape
    whole = jax.ShapeDtypeStruct((tokens, width), jnp.bfloat16)
    return pl.pallas_call(
        norm_kernel,
        out_shape=(whole, whole),
        cost_estimate=pl.CostEstimate(
            flops=8 * tokens * width, bytes_accessed=14 * tokens * width, transcendentals=tokens
        ),
        name="norm",
    )(keep, got, residual, gain[None, :])


def attend_kernel(outers, first, last, info, q_ref, *refs):
    count = 2 if last else len(outers)
    pieces, refs = refs[:count], refs[count:]
    if not first:
        top_in, total_in, acc_in, *refs = refs
    if last:
        out_ref, *refs = refs
    else:
        top_out, total_out, acc_out, *refs = refs
    kv_scr, turned, top, total, acc, sems = refs
    y, x, c = info[0], info[1], info[2]
    chip = y * SIDE + x
    block = 256
    group = pl.program_id(0) // 2

    def copies(at):
        made = []
        for inner in range(SIDE):
            piece, row = locate(outers[at], inner, block + TOLD_ROWS)
            source = pieces[piece - outers[0]].at[pl.ds(row, block)]
            target = kv_scr.at[at, pl.ds(inner * block, block)]
            made.append(pltpu.make_async_copy(source, target, sems.at[at, inner]))
        return made

    def turn(at):
        columns = pl.ds(pl.multiple_of((2 * group + 1) * HEAD_DIM, HEAD_DIM), HEAD_DIM)
        for inner in range(SIDE):
            rows = pl.ds(inner * block, block)
            value = kv_scr[at, rows, columns].astype(jnp.float32)
            turned[at, :, inner * block : (inner + 1) * block] = value.T.astype(jnp.bfloat16)

    @pl.when(pl.program_id(0) == 0)
    def _():
        for at in range(len(outers)):
            for copy in copies(at):
                copy.start()
        for at in range(len(outers)):
            for copy in copies(at):
                copy.wait()
            turn(at)

    @pl.when(pl.program_id(0) == 2)
    def _():
        for at in range(len(outers)):
            turn(at)

    scale = HEAD_DIM ** (-0.5) * LOG2E
    heads = q_ref.shape[1] // HEAD_DIM
    q = jnp.concatenate(
        [q_ref[:, h * HEAD_DIM : (h + 1) * HEAD_DIM] for h in range(heads)], axis=0
    )
    if not first:
        top[...], total[...], acc[...] = top_in[0], total_in[0], acc_in[0]
    else:
        top[...] = jnp.full(top.shape, -1e30, jnp.float32)
        total[...] = jnp.zeros(total.shape, jnp.float32)
        acc[...] = jnp.zeros(acc.shape, jnp.float32)

    def step(at, key):
        columns = pl.ds(pl.multiple_of(2 * group * HEAD_DIM, HEAD_DIM), HEAD_DIM)
        s = (
            lax.dot_general(
                kv_scr[at, :, columns],
                q,
                (((1,), (1,)), ((), ())),
                preferred_element_type=jnp.float32,
            )
            * scale
        )
        if key is not None:
            query = lax.broadcasted_iota(jnp.int32, (1, s.shape[1]), 1) % block + chip * block
            s = jnp.where(key <= query, s, -1e30)
        old = top[...]
        new = jnp.maximum(old, jnp.max(s, axis=0, keepdims=True))
        p = jnp.exp2(s - new)
        shrink = jnp.exp2(old - new)
        top[...] = new
        total[...] = total[...] * shrink + jnp.sum(p, axis=0, keepdims=True)
        acc[...] = acc[...] * shrink + jnp.dot(
            turned[at], p.astype(jnp.bfloat16), preferred_element_type=jnp.float32
        )

    @pl.loop(0, len(outers))
    def _(at):
        offset = jnp.where(at == 0, OFFSETS[outers[0]], OFFSETS[outers[-1]])
        line_y = lax.rem(y + offset + SIDE, SIDE)
        line_x = lax.rem(x + offset + SIDE, SIDE)
        least = jnp.where(c == 0, line_y * SIDE, line_x)
        most = jnp.where(c == 0, line_y * SIDE + SIDE - 1, CHIPS - SIDE + line_x)

        @pl.when(most < chip)
        def _():
            step(at, None)

        @pl.when((most >= chip) & (least <= chip))
        def _():
            homes = []
            for inner in range(SIDE):
                other = OFFSETS[inner] + SIDE
                home = jnp.where(
                    c == 0,
                    line_y * SIDE + lax.rem(x + other, SIDE),
                    lax.rem(y + other, SIDE) * SIDE + line_x,
                )
                homes.append(lax.broadcasted_iota(jnp.int32, (block, 1), 0) + home * block)
            step(at, jnp.concatenate(homes, axis=0))

    if last:
        out = (acc[...] / total[...]).T.astype(jnp.bfloat16)
        for h in range(heads):
            out_ref[:, h * HEAD_DIM : (h + 1) * HEAD_DIM] = out[h * block : (h + 1) * block]
    else:
        top_out[0], total_out[0], acc_out[0] = top[...], total[...], acc[...]


def attend(info, q, pieces, outers, carried=()):
    tokens, width = q.shape
    steps = 4
    at_once = width // steps
    first, last = outers[0] == 0, outers[-1] == 3
    columns = at_once // HEAD_DIM * tokens
    q_spec = pl.BlockSpec((tokens, at_once), lambda i, info: (0, i))
    shapes = [(1, columns), (1, columns), (HEAD_DIM, columns)]
    specs = [pl.BlockSpec((1, *shape), lambda i, info: (i, 0, 0)) for shape in shapes]
    sums = [jax.ShapeDtypeStruct((steps, *shape), jnp.float32) for shape in shapes]
    keys = SIDE * tokens
    lines = len(outers)
    return pl.pallas_call(
        functools.partial(attend_kernel, outers, first, last),
        out_shape=jax.ShapeDtypeStruct((tokens, width), jnp.bfloat16) if last else sums,
        grid_spec=pltpu.PrefetchScalarGridSpec(
            num_scalar_prefetch=1,
            grid=(steps,),
            in_specs=[q_spec] + [ANY] * len(pieces) + specs[: len(carried)],
            out_specs=q_spec if last else specs,
            scratch_shapes=[
                pltpu.VMEM((lines, keys, 4 * HEAD_DIM), jnp.bfloat16),
                pltpu.VMEM((lines, HEAD_DIM, keys), jnp.bfloat16),
                *(pltpu.VMEM(shape, jnp.float32) for shape in shapes),
                pltpu.SemaphoreType.DMA((lines, SIDE)),
            ],
        ),
        compiler_params=pltpu.CompilerParams(vmem_limit_bytes=VMEM_LIMIT),
        cost_estimate=pl.CostEstimate(
            flops=4 * tokens * width * keys * lines,
            bytes_accessed=6 << 20,
            transcendentals=tokens * width * keys * lines // HEAD_DIM,
        ),
        name="attend_%d" % outers[0],
    )(info, q, *pieces, *carried)


def project_kernel(info, *refs):
    part, w_ref = refs[:2]
    keep_ref, send_ref, w_scr, sems = refs[-4:]
    c = info[2]
    depth, width = part.shape[1], w_ref.shape[1]
    tokens = keep_ref.shape[0]

    own = pl.ds(pl.multiple_of(c * tokens, tokens), tokens)
    other = pl.ds(pl.multiple_of((1 - c) * tokens, tokens), tokens)
    tiles = w_scr.shape[0]
    tile = width // tiles

    def copy_of(i):
        source = w_ref.at[pl.ds(pl.multiple_of(c * depth, depth), depth), pl.ds(i * tile, tile)]
        return pltpu.make_async_copy(source, w_scr.at[i], sems.at[i])

    for i in range(tiles):
        copy_of(i).start()
    for i in range(tiles):
        copy_of(i).wait()
        for rows, target in ((other, send_ref), (own, keep_ref)):
            product = jnp.dot(part[rows, :], w_scr[i], preferred_element_type=jnp.float32)
            target[:, i * tile : (i + 1) * tile] = product.astype(target.dtype)


def project(info, attended, weight, behind):
    width = weight.shape[1]
    tokens, depth = attended.shape[0] // CORES, attended.shape[1]
    tiles = 8
    vmem = pl.BlockSpec(memory_space=pltpu.VMEM)
    return pl.pallas_call(
        project_kernel,
        out_shape=(
            jax.ShapeDtypeStruct((tokens, width), jnp.float32),
            jax.ShapeDtypeStruct((tokens, width), jnp.bfloat16),
        ),
        in_specs=[pl.BlockSpec(memory_space=pltpu.SMEM), vmem, ANY] + [ANY] * len(behind),
        out_specs=(vmem, vmem),
        scratch_shapes=[
            pltpu.VMEM((tiles, depth, width // tiles), jnp.bfloat16),
            pltpu.SemaphoreType.DMA((tiles,)),
        ],
        compiler_params=pltpu.CompilerParams(vmem_limit_bytes=VMEM_LIMIT),
        cost_estimate=pl.CostEstimate(
            flops=4 * tokens * width * depth, bytes_accessed=12 << 20, transcendentals=0
        ),
        name="project",
    )(info, attended, weight, *behind)


def expert_kernel(outers, behind, info, *refs):
    pair_count = 2 * len(outers)
    count = 2 if outers[-1] == 3 else len(outers)
    told, weights, refs = refs[:count], (refs[count : count + 3], refs[count + 3 : count + 6]), refs[count + 6 :]
    pieces, refs = refs[:count], refs[count + behind :]
    outs, refs = refs[:pair_count], refs[pair_count:]
    told_scr, pick_scr, put_scr, share_scr, x_scr, h_scr, hid_scr, y_scr = refs[:8]
    gate_scr, up_scr, down_scr, told_sems, in_sems, out_sems, w_sems = refs[8:]
    _, pair_rows, pair_tokens = pick_scr.shape
    experts = 4
    slots = pair_rows // experts
    block = pair_tokens // 2
    width = x_scr.shape[2]
    half = width // 2
    buffers = (gate_scr, up_scr, down_scr)

    def weight_copy(e, which):
        source = weights[e // 2][which].at[e % 2]
        return pltpu.make_async_copy(
            source, buffers[which].at[e % 2], w_sems.at[which, e % 2]
        )

    def load(pair):
        piece, row = locate(outers[pair // 2], pair % 2 * 2, block)
        source = pieces[piece - outers[0]].at[pl.ds(row, pair_tokens)]
        return pltpu.make_async_copy(source, x_scr.at[pair], in_sems.at[pair])

    def store(pair):
        return pltpu.make_async_copy(x_scr.at[pair], outs[pair], out_sems.at[pair])

    told_copies = []
    for at, outer in enumerate(outers):
        for inner in range(SIDE):
            piece, row = locate(outer, inner, CORES * block + TOLD_ROWS)
            number = at * SIDE + inner
            told_copies.append(
                pltpu.make_async_copy(
                    told[piece - outers[0]].at[pl.ds(row + CORES * block, TOLD_ROWS)],
                    told_scr.at[number],
                    told_sems.at[number],
                )
            )
    for copy in told_copies:
        copy.start()
    for pair in range(pair_count):
        load(pair).start()
    for which in range(3):
        weight_copy(0, which).start()
    for copy in told_copies:
        copy.wait()

    first_expert = (info[0] * SIDE + info[1]) * experts
    own_first = 2 * info[2]

    def routes_of(number, at):
        rows = told_scr[number].astype(jnp.float32)
        expert, rank, high, mid = (rows[:TOPK, i * block : (i + 1) * block] for i in range(4))
        share = high + mid + rows[TOPK:, :block]
        local = expert.astype(jnp.int32) - first_expert
        here = (local >= 0) & (local < experts)
        local = local - own_first
        local = jnp.where(local < 0, local + experts, local)
        row = local * slots + at * (slots // 2) + rank.astype(jnp.int32)
        return jnp.where(here, row, -1), share

    @pl.loop(0, pair_count)
    def _(pair):
        row, share = zip(*(routes_of(2 * pair + at, at) for at in range(2)))
        row, share = jnp.concatenate(row, axis=1), jnp.concatenate(share, axis=1)
        slot = lax.broadcasted_iota(jnp.int32, (pair_rows, pair_tokens), 0)
        pick = jnp.zeros(slot.shape, jnp.float32)
        shares = jnp.zeros(slot.shape, jnp.float32)
        for r in range(TOPK):
            match = row[r : r + 1, :] == slot
            pick = jnp.where(match, 1.0, pick)
            shares = jnp.where(match, share[r : r + 1, :], shares)
        pick_scr[pair] = pick.astype(jnp.bfloat16)
        put_scr[pair] = pick.T.astype(jnp.bfloat16)
        share_scr[pair] = jnp.sum(shares, axis=1, keepdims=True)

    for pair in range(pair_count):
        load(pair).wait()
        for part in range(2):
            columns = pl.ds(part * half, half)
            rows = jnp.dot(
                pick_scr[pair], x_scr[pair, :, columns], preferred_element_type=jnp.float32
            ).astype(jnp.bfloat16)
            for e in range(experts):
                h_scr[e, pl.ds(pair * slots, slots), columns] = rows[e * slots : (e + 1) * slots]

    for which in range(3):
        weight_copy(1, which).start()
    tile, wide_tile = 256, 512

    @pl.loop(0, experts)
    def _(e):
        at = lax.rem(e, 2)

        def wait(which):
            pltpu.make_async_copy(
                weights[0][which].at[0], buffers[which].at[at], w_sems.at[which, at]
            ).wait()

        def fetch(which):
            @pl.when(e < 2)
            def _():
                pltpu.make_async_copy(
                    weights[1][which].at[at], buffers[which].at[at], w_sems.at[which, at]
                ).start()

        wait(0)
        wait(1)
        for begin in range(0, hid_scr.shape[1], tile):
            columns = pl.ds(begin, tile)
            gate = jnp.dot(h_scr[e], gate_scr[at, :, columns], preferred_element_type=jnp.float32)
            up = jnp.dot(h_scr[e], up_scr[at, :, columns], preferred_element_type=jnp.float32)
            hid_scr[:, columns] = (gate / (1.0 + jnp.exp(-gate)) * up).astype(jnp.bfloat16)
        fetch(0)
        fetch(1)
        wait(2)
        for begin in range(0, width, wide_tile):
            columns = pl.ds(begin, wide_tile)
            rows = jnp.dot(hid_scr[...], down_scr[at, :, columns], preferred_element_type=jnp.float32)
            for pair in range(pair_count):
                slot_rows = pl.ds(pl.multiple_of(e * slots, slots), slots)
                y_scr[pair, slot_rows, columns] = (
                    rows[pair * slots : (pair + 1) * slots] * share_scr[pair, slot_rows, :]
                ).astype(jnp.bfloat16)
        fetch(2)

    for pair in reversed(range(pair_count)):
        for part in range(2):
            columns = pl.ds(part * half, half)
            x_scr[pair, :, columns] = jnp.dot(
                put_scr[pair], y_scr[pair, :, columns], preferred_element_type=jnp.float32
            ).astype(jnp.bfloat16)
        store(pair).start()
    for pair in range(pair_count):
        store(pair).wait()


def run_experts(info, told, own, sib, pieces, outers, behind=()):
    width, hidden = own[0].shape[1:]
    experts = 4
    pair_count = 2 * len(outers)
    pair_tokens = pieces[0].shape[0] // (1 if outers[-1] == 3 else 2)
    slots = 3 * pair_tokens * TOPK // (2 * experts * CHIPS)
    pair_rows = experts * slots
    rows = pair_count * slots
    return pl.pallas_call(
        functools.partial(expert_kernel, outers, len(behind)),
        out_shape=[jax.ShapeDtypeStruct((pair_tokens, width), jnp.bfloat16)] * pair_count,
        in_specs=[pl.BlockSpec(memory_space=pltpu.SMEM)] + [ANY] * (6 + 2 * len(pieces) + len(behind)),
        out_specs=[ANY] * pair_count,
        scratch_shapes=[
            pltpu.VMEM((2 * pair_count, TOLD_ROWS, told[0].shape[1]), jnp.bfloat16),
            pltpu.VMEM((pair_count, pair_rows, pair_tokens), jnp.bfloat16),
            pltpu.VMEM((pair_count, pair_tokens, pair_rows), jnp.bfloat16),
            pltpu.VMEM((pair_count, pair_rows, 1), jnp.float32),
            pltpu.VMEM((pair_count, pair_tokens, width), jnp.bfloat16),
            pltpu.VMEM((experts, rows, width), jnp.bfloat16),
            pltpu.VMEM((rows, hidden), jnp.bfloat16),
            pltpu.VMEM((pair_count, pair_rows, width), jnp.bfloat16),
            pltpu.VMEM((2, width, hidden), jnp.bfloat16),
            pltpu.VMEM((2, width, hidden), jnp.bfloat16),
            pltpu.VMEM((2, hidden, width), jnp.bfloat16),
            pltpu.SemaphoreType.DMA((2 * pair_count,)),
            pltpu.SemaphoreType.DMA((pair_count,)),
            pltpu.SemaphoreType.DMA((pair_count,)),
            pltpu.SemaphoreType.DMA((3, 2)),
        ],
        compiler_params=pltpu.CompilerParams(vmem_limit_bytes=VMEM_LIMIT),
        cost_estimate=pl.CostEstimate(
            flops=6 * experts * rows * width * hidden,
            bytes_accessed=56 << 20,
            transcendentals=experts * rows * hidden,
        ),
        name="experts_%d" % outers[0],
    )(info, *told, *own, *sib, *pieces, *behind)


def told_routes(routes, route_gates, experts_all):
    tokens = routes.shape[0]
    share = route_gates / jnp.sum(route_gates, axis=1, keepdims=True)
    named = (routes[:, :, None] == jnp.arange(experts_all, dtype=jnp.int32)).astype(jnp.float32)
    hits = jnp.sum(named, axis=1)
    order = jnp.arange(tokens)
    earlier = (order[None, :] < order[:, None]).astype(jnp.bfloat16)
    rank = jnp.dot(earlier, hits.astype(jnp.bfloat16), preferred_element_type=jnp.float32)
    rank = jnp.sum(named * rank[:, None, :], axis=2)
    high = share.astype(jnp.bfloat16)
    left = share - high.astype(jnp.float32)
    mid = left.astype(jnp.bfloat16)
    low = (left - mid.astype(jnp.float32)).astype(jnp.bfloat16)
    first = jnp.concatenate([routes.astype(jnp.bfloat16).T, rank.astype(jnp.bfloat16).T, high.T, mid.T], axis=1)
    return jnp.concatenate([first, jnp.pad(low.T, ((0, 0), (0, 3 * tokens)))], axis=0)


def in_order(c, mine, theirs):
    return jnp.where(
        c == 0, jnp.concatenate([mine, theirs], axis=0), jnp.concatenate([theirs, mine], axis=0)
    )


def body(
    queries,
    key_vectors,
    value_vectors,
    residual,
    out_weight,
    norm_gain,
    routes,
    route_gates,
    w_gate,
    w_up,
    w_down,
):
    me = lax.axis_index("seq")
    c = me % CORES
    x = me // CORES % SIDE
    y = me // (CORES * SIDE)
    info = jnp.stack([y, x, c]).astype(jnp.int32)
    tokens, width = residual.shape
    experts_all = w_gate.shape[0] * lax.axis_size("seq")

    kv_half = key_vectors.shape[1] // 2
    q_half = queries.shape[1] // 2

    def half_of(array, which, size):
        return lax.dynamic_slice_in_dim(array, which * size, size, axis=1)

    def kv_of(which):
        k, v = (half_of(a, which, kv_half) for a in (key_vectors, value_vectors))
        d = HEAD_DIM
        return jnp.concatenate([k[:, :d], v[:, :d], k[:, d:], v[:, d:]], axis=1)

    kv_send, q_send = together(kv_of(1 - c), half_of(queries, 1 - c, q_half))
    kv = in_order(c, kv_of(c), to_sibling(kv_send))
    q_got = to_sibling(q_send)
    told = told_routes(routes, route_gates, experts_all)
    kv = jnp.concatenate([kv, told], axis=0)

    weight = lax.all_gather(out_weight, "seq", axis=0, tiled=True)
    own = (w_gate, w_up, w_down)

    line = gather_near(kv)
    before, after = gather_wide(line)
    q = in_order(c, half_of(queries, c, q_half), q_got)
    sums = attend(info, q, [line], (0,))
    wide_done, far = gather_far(before, after, sums[:1])
    *sends, _ = together(*own, wide_done)
    sib = [to_sibling(w) for w in sends]
    sums = attend(info, q, [before, after], (1, 2), sums)
    attended = attend(info, q, far, (3,), sums)
    keep, send = project(info, attended, weight, sib)
    stream, normed = norm(keep, to_sibling(send), residual, norm_gain)
    told_near, told_far = [line, before, after], far
    line = gather_near(normed)
    before, after = gather_wide(line)
    partial = run_experts(info, told_near[:1], own, sib, [line], (0,))
    _, far = gather_far(before, after, partial[:1])
    partial += run_experts(info, told_near[1:], own, sib, [before, after], (1, 2))
    partial += run_experts(info, told_far, own, sib, far, (3,), partial[2:3])
    expert_sum = scatter_grid(partial)
    layer_out = (stream.astype(jnp.float32) + expert_sum).astype(jnp.bfloat16)
    return (stream, layer_out)


def solution(mesh):
    in_specs = (
        P(("dp", "seq"), None),
        P(("dp", "seq"), None),
        P(("dp", "seq"), None),
        P(("dp", "seq"), None),
        P("seq", None),
        P(),
        P(("dp", "seq"), None),
        P(("dp", "seq"), None),
        P("seq", None, None),
        P("seq", None, None),
        P("seq", None, None),
    )
    out_specs = (P(("dp", "seq"), None), P(("dp", "seq"), None))
    return jax.shard_map(body, mesh=mesh, in_specs=in_specs, out_specs=out_specs, check_vma=False)
```

```python
import functools

import jax
import jax.numpy as jnp
from jax import lax
from jax.experimental import pallas as pl
from jax.experimental.pallas import tpu as pltpu
from jax.sharding import PartitionSpec as P

HEADS = 32
KV_HEADS = 4
HEAD_DIM = 128
TOPK = 8
SIDE = 4
CHIPS = SIDE * SIDE
CORES = 2
OFFSETS = (0, -1, 1, 2)
TOLD_ROWS = 16
LOG2E = 1.4426950408889634
ANY = pl.BlockSpec(memory_space=pl.ANY)
VMEM_LIMIT = 60 * 1024 * 1024


def ring_pairs(stage, step):
    pairs = []
    for y in range(SIDE):
        for x in range(SIDE):
            for c in range(CORES):
                dy, dx = (step, 0) if stage != c else (0, step)
                source = (y * SIDE + x) * CORES + c
                target = ((y + dy) % SIDE * SIDE + (x + dx) % SIDE) * CORES + c
                pairs.append((source, target))
    return pairs


def along(value, stage, step):
    return lax.ppermute(value, "seq", ring_pairs(stage, step))


def to_sibling(value):
    devices = CHIPS * CORES
    return lax.ppermute(value, "seq", [(d, d ^ 1) for d in range(devices)])


def together(*values):
    return lax.optimization_barrier(values)


def rearrange(sources, plan, name, behind=()):
    width = sources[0].shape[1]

    def kernel(*refs):
        ins, outs = refs[: len(sources)], refs[len(sources) + len(behind) :]
        for out, parts in zip(outs, plan):
            at = 0
            for source, begin, rows in parts:
                out[at : at + rows, :] = ins[source][begin : begin + rows, :]
                at += rows

    rows_out = [sum(rows for _, _, rows in parts) for parts in plan]
    return pl.pallas_call(
        kernel,
        out_shape=[jax.ShapeDtypeStruct((rows, width), sources[0].dtype) for rows in rows_out],
        in_specs=[pl.BlockSpec(memory_space=pltpu.VMEM)] * len(sources) + [ANY] * len(behind),
        compiler_params=pltpu.CompilerParams(vmem_limit_bytes=24 * 1024 * 1024),
        cost_estimate=pl.CostEstimate(
            flops=0, bytes_accessed=4 * width * sum(rows_out), transcendentals=0
        ),
        name=name,
    )(*sources, *behind)


def gather_near(block, pieces):
    rows = block.shape[0]
    got = [along(block, 0, step) for step in (1, -1, 2)]
    each = SIDE // pieces
    plan = [[(i, 0, rows) for i in range(p * each, (p + 1) * each)] for p in range(pieces)]
    return rearrange([block, *got], plan, "line")


def gather_wide(line):
    before = [along(piece, 1, 1) for piece in line]
    after = [along(piece, 1, -1) for piece in line]
    return before + after


def gather_far(wide, behind):
    if len(wide) == 4:
        low, high, *_ = together(wide[0], wide[3], *behind)
    else:
        half = wide[0].shape[0] // 2
        low, high = rearrange(wide, [[(0, 0, half)], [(1, half, half)]], "halves", behind)
    return low, [along(low, 1, 1), along(high, 1, -1)]


def locate(lines, pieces, at, inner, rows):
    if pieces == lines:
        return at, inner * rows
    return 2 * at + inner // 2, (inner % 2) * rows


def add(*terms):
    return functools.reduce(jnp.add, [term.astype(jnp.float32) for term in terms])


def add_kernel(a_ref, b_ref, c_ref, d_ref, low_ref, high_ref):
    low_ref[...] = add(a_ref[...], b_ref[...]).astype(low_ref.dtype)
    high_ref[...] = add(c_ref[...], d_ref[...]).astype(high_ref.dtype)


def add_pairs(*terms):
    shape = jax.ShapeDtypeStruct(terms[0].shape, terms[0].dtype)
    return pl.pallas_call(
        add_kernel,
        out_shape=(shape, shape),
        compiler_params=pltpu.CompilerParams(vmem_limit_bytes=24 * 1024 * 1024),
        cost_estimate=pl.CostEstimate(
            flops=2 * terms[0].size, bytes_accessed=12 * terms[0].size, transcendentals=0
        ),
        name="add_pairs",
    )(*terms)


def scatter_grid(halves):
    rounded = jnp.bfloat16
    own_low, own_high, before_low, before_high, after_low, after_high, far_low, far_high = halves
    early_high, early_low = along(after_high, 1, 1), along(before_low, 1, -1)
    far_low, far_high, early_high, early_low = together(far_low, far_high, early_high, early_low)
    got_low, got_high = along(far_low, 1, 1), along(far_high, 1, -1)
    low, high = add_pairs(after_low, got_low, before_high, got_high)
    late_low, late_high = along(low, 1, 1), along(high, 1, -1)
    low = add(own_low, late_low, early_low).astype(rounded)
    high = add(own_high, early_high, late_high).astype(rounded)
    rows = low.shape[0] // 2
    own, before, after, far = low[:rows], low[rows:], high[:rows], high[rows:]
    return add(own, along(after, 0, 1), along(before, 0, -1), along(far, 0, 2))


def norm_kernel(keep_ref, got_ref, residual_ref, gain_ref, stream_ref, normed_ref):
    attn_sum = keep_ref[...] + got_ref[...].astype(jnp.float32)
    stream = (residual_ref[...].astype(jnp.float32) + attn_sum).astype(jnp.bfloat16)
    stream_ref[...] = stream
    stream = stream.astype(jnp.float32)
    mean = jnp.mean(stream * stream, axis=1, keepdims=True)
    normed_ref[...] = (stream * lax.rsqrt(mean + 1e-06) * gain_ref[...]).astype(jnp.bfloat16)


def norm(keep, got, residual, gain):
    tokens, width = residual.shape
    whole = jax.ShapeDtypeStruct((tokens, width), jnp.bfloat16)
    return pl.pallas_call(
        norm_kernel,
        out_shape=(whole, whole),
        cost_estimate=pl.CostEstimate(
            flops=8 * tokens * width, bytes_accessed=14 * tokens * width, transcendentals=tokens
        ),
        name="norm",
    )(keep, got, residual, gain[None, :])


def attend_kernel(outers, count, first, last, info, q_ref, *refs):
    pieces, refs = refs[:count], refs[count:]
    if not first:
        top_in, total_in, acc_in, *refs = refs
    if last:
        out_ref, *refs = refs
    else:
        top_out, total_out, acc_out, *refs = refs
    kv_scr, turned, top, total, acc, sems = refs
    y, x, c = info[0], info[1], info[2]
    chip = y * SIDE + x
    block = 256
    group = pl.program_id(0) // 2

    def copies(at):
        made = []
        for inner in range(SIDE):
            piece, row = locate(len(outers), count, at, inner, block + TOLD_ROWS)
            source = pieces[piece].at[pl.ds(row, block)]
            target = kv_scr.at[at, pl.ds(inner * block, block)]
            made.append(pltpu.make_async_copy(source, target, sems.at[at, inner]))
        return made

    def turn(at):
        columns = pl.ds(pl.multiple_of((2 * group + 1) * HEAD_DIM, HEAD_DIM), HEAD_DIM)
        for inner in range(SIDE):
            rows = pl.ds(inner * block, block)
            value = kv_scr[at, rows, columns].astype(jnp.float32)
            turned[at, :, inner * block : (inner + 1) * block] = value.T.astype(jnp.bfloat16)

    @pl.when(pl.program_id(0) == 0)
    def _():
        for at in range(len(outers)):
            for copy in copies(at):
                copy.start()
        for at in range(len(outers)):
            for copy in copies(at):
                copy.wait()
            turn(at)

    @pl.when(pl.program_id(0) == 2)
    def _():
        for at in range(len(outers)):
            turn(at)

    scale = HEAD_DIM ** (-0.5) * LOG2E
    heads = q_ref.shape[1] // HEAD_DIM
    q = jnp.concatenate(
        [q_ref[:, h * HEAD_DIM : (h + 1) * HEAD_DIM] for h in range(heads)], axis=0
    )
    if not first:
        top[...], total[...], acc[...] = top_in[0], total_in[0], acc_in[0]
    else:
        top[...] = jnp.full(top.shape, -1e30, jnp.float32)
        total[...] = jnp.zeros(total.shape, jnp.float32)
        acc[...] = jnp.zeros(acc.shape, jnp.float32)

    def step(at, key):
        columns = pl.ds(pl.multiple_of(2 * group * HEAD_DIM, HEAD_DIM), HEAD_DIM)
        s = (
            lax.dot_general(
                kv_scr[at, :, columns],
                q,
                (((1,), (1,)), ((), ())),
                preferred_element_type=jnp.float32,
            )
            * scale
        )
        if key is not None:
            query = lax.broadcasted_iota(jnp.int32, (1, s.shape[1]), 1) % block + chip * block
            s = jnp.where(key <= query, s, -1e30)
        old = top[...]
        new = jnp.maximum(old, jnp.max(s, axis=0, keepdims=True))
        p = jnp.exp2(s - new)
        shrink = jnp.exp2(old - new)
        top[...] = new
        total[...] = total[...] * shrink + jnp.sum(p, axis=0, keepdims=True)
        acc[...] = acc[...] * shrink + jnp.dot(
            turned[at], p.astype(jnp.bfloat16), preferred_element_type=jnp.float32
        )

    @pl.loop(0, len(outers))
    def _(at):
        offset = jnp.where(at == 0, OFFSETS[outers[0]], OFFSETS[outers[-1]])
        line_y = lax.rem(y + offset + SIDE, SIDE)
        line_x = lax.rem(x + offset + SIDE, SIDE)
        least = jnp.where(c == 0, line_y * SIDE, line_x)
        most = jnp.where(c == 0, line_y * SIDE + SIDE - 1, CHIPS - SIDE + line_x)

        @pl.when(most < chip)
        def _():
            step(at, None)

        @pl.when((most >= chip) & (least <= chip))
        def _():
            homes = []
            for inner in range(SIDE):
                other = OFFSETS[inner] + SIDE
                home = jnp.where(
                    c == 0,
                    line_y * SIDE + lax.rem(x + other, SIDE),
                    lax.rem(y + other, SIDE) * SIDE + line_x,
                )
                homes.append(lax.broadcasted_iota(jnp.int32, (block, 1), 0) + home * block)
            step(at, jnp.concatenate(homes, axis=0))

    if last:
        out = (acc[...] / total[...]).T.astype(jnp.bfloat16)
        for h in range(heads):
            out_ref[:, h * HEAD_DIM : (h + 1) * HEAD_DIM] = out[h * block : (h + 1) * block]
    else:
        top_out[0], total_out[0], acc_out[0] = top[...], total[...], acc[...]


def attend(info, q, pieces, outers, carried=()):
    tokens, width = q.shape
    steps = 4
    at_once = width // steps
    first, last = outers[0] == 0, outers[-1] == 3
    columns = at_once // HEAD_DIM * tokens
    q_spec = pl.BlockSpec((tokens, at_once), lambda i, info: (0, i))
    shapes = [(1, columns), (1, columns), (HEAD_DIM, columns)]
    specs = [pl.BlockSpec((1, *shape), lambda i, info: (i, 0, 0)) for shape in shapes]
    sums = [jax.ShapeDtypeStruct((steps, *shape), jnp.float32) for shape in shapes]
    keys = SIDE * tokens
    lines = len(outers)
    return pl.pallas_call(
        functools.partial(attend_kernel, outers, len(pieces), first, last),
        out_shape=jax.ShapeDtypeStruct((tokens, width), jnp.bfloat16) if last else sums,
        grid_spec=pltpu.PrefetchScalarGridSpec(
            num_scalar_prefetch=1,
            grid=(steps,),
            in_specs=[q_spec] + [ANY] * len(pieces) + specs[: len(carried)],
            out_specs=q_spec if last else specs,
            scratch_shapes=[
                pltpu.VMEM((lines, keys, 4 * HEAD_DIM), jnp.bfloat16),
                pltpu.VMEM((lines, HEAD_DIM, keys), jnp.bfloat16),
                *(pltpu.VMEM(shape, jnp.float32) for shape in shapes),
                pltpu.SemaphoreType.DMA((lines, SIDE)),
            ],
        ),
        compiler_params=pltpu.CompilerParams(vmem_limit_bytes=VMEM_LIMIT),
        cost_estimate=pl.CostEstimate(
            flops=4 * tokens * width * keys * lines,
            bytes_accessed=6 << 20,
            transcendentals=tokens * width * keys * lines // HEAD_DIM,
        ),
        name="attend_%d" % outers[0],
    )(info, q, *pieces, *carried)


def project_kernel(info, *refs):
    part, w_ref = refs[:2]
    keep_ref, send_ref, w_scr, sems = refs[-4:]
    c = info[2]
    depth, width = part.shape[1], w_ref.shape[1]
    tokens = keep_ref.shape[0]

    own = pl.ds(pl.multiple_of(c * tokens, tokens), tokens)
    other = pl.ds(pl.multiple_of((1 - c) * tokens, tokens), tokens)
    tiles = w_scr.shape[0]
    tile = width // tiles

    def copy_of(i):
        source = w_ref.at[pl.ds(pl.multiple_of(c * depth, depth), depth), pl.ds(i * tile, tile)]
        return pltpu.make_async_copy(source, w_scr.at[i], sems.at[i])

    for i in range(tiles):
        copy_of(i).start()
    for i in range(tiles):
        copy_of(i).wait()
        for rows, target in ((other, send_ref), (own, keep_ref)):
            product = jnp.dot(part[rows, :], w_scr[i], preferred_element_type=jnp.float32)
            target[:, i * tile : (i + 1) * tile] = product.astype(target.dtype)


def project(info, attended, weight, behind):
    width = weight.shape[1]
    tokens, depth = attended.shape[0] // CORES, attended.shape[1]
    tiles = 4
    vmem = pl.BlockSpec(memory_space=pltpu.VMEM)
    return pl.pallas_call(
        project_kernel,
        out_shape=(
            jax.ShapeDtypeStruct((tokens, width), jnp.float32),
            jax.ShapeDtypeStruct((tokens, width), jnp.bfloat16),
        ),
        in_specs=[pl.BlockSpec(memory_space=pltpu.SMEM), vmem, ANY] + [ANY] * len(behind),
        out_specs=(vmem, vmem),
        scratch_shapes=[
            pltpu.VMEM((tiles, depth, width // tiles), jnp.bfloat16),
            pltpu.SemaphoreType.DMA((tiles,)),
        ],
        compiler_params=pltpu.CompilerParams(vmem_limit_bytes=VMEM_LIMIT),
        cost_estimate=pl.CostEstimate(
            flops=4 * tokens * width * depth, bytes_accessed=12 << 20, transcendentals=0
        ),
        name="project",
    )(info, attended, weight, *behind)


def expert_kernel(outers, told_count, behind, info, *refs):
    pair_count = 2 * len(outers)
    count = pair_count
    told, refs = refs[:told_count], refs[told_count:]
    weights, refs = (refs[:3], refs[3:6]), refs[6:]
    pieces, refs = refs[:count], refs[count + behind :]
    outs, refs = refs[:pair_count], refs[pair_count:]
    told_scr, pick_scr, put_scr, share_scr, x_scr, h_scr, hid_scr, y_scr = refs[:8]
    gate_scr, up_scr, down_scr, told_sems, in_sems, out_sems, w_sems = refs[8:]
    _, pair_rows, pair_tokens = pick_scr.shape
    experts = 4
    slots = pair_rows // experts
    block = pair_tokens // 2
    width = x_scr.shape[2]
    half = width // 2
    buffers = (gate_scr, up_scr, down_scr)

    def weight_copy(e, which):
        source = weights[e // 2][which].at[e % 2]
        return pltpu.make_async_copy(source, buffers[which].at[e], w_sems.at[which, e])

    def load(pair):
        return pltpu.make_async_copy(pieces[pair], x_scr.at[pair], in_sems.at[pair])

    def store(pair):
        return pltpu.make_async_copy(x_scr.at[pair], outs[pair], out_sems.at[pair])

    told_copies = []
    for at in range(len(outers)):
        for inner in range(SIDE):
            piece, row = locate(len(outers), told_count, at, inner, CORES * block + TOLD_ROWS)
            number = at * SIDE + inner
            told_copies.append(
                pltpu.make_async_copy(
                    told[piece].at[pl.ds(row + CORES * block, TOLD_ROWS)],
                    told_scr.at[number],
                    told_sems.at[number],
                )
            )
    for copy in told_copies:
        copy.start()
    for pair in range(pair_count):
        load(pair).start()
    for which in range(3):
        weight_copy(0, which).start()
    for copy in told_copies:
        copy.wait()

    first_expert = (info[0] * SIDE + info[1]) * experts
    own_first = 2 * info[2]

    def routes_of(number, at):
        rows = told_scr[number].astype(jnp.float32)
        expert, rank, high, mid = (rows[:TOPK, i * block : (i + 1) * block] for i in range(4))
        share = high + mid + rows[TOPK:, :block]
        local = expert.astype(jnp.int32) - first_expert
        here = (local >= 0) & (local < experts)
        local = local - own_first
        local = jnp.where(local < 0, local + experts, local)
        row = local * slots + at * (slots // 2) + rank.astype(jnp.int32)
        return jnp.where(here, row, -1), share

    @pl.loop(0, pair_count)
    def _(pair):
        row, share = zip(*(routes_of(2 * pair + at, at) for at in range(2)))
        row, share = jnp.concatenate(row, axis=1), jnp.concatenate(share, axis=1)
        slot = lax.broadcasted_iota(jnp.int32, (pair_rows, pair_tokens), 0)
        pick = jnp.zeros(slot.shape, jnp.float32)
        shares = jnp.zeros(slot.shape, jnp.float32)
        for r in range(TOPK):
            match = row[r : r + 1, :] == slot
            pick = jnp.where(match, 1.0, pick)
            shares = jnp.where(match, share[r : r + 1, :], shares)
        pick_scr[pair] = pick.astype(jnp.bfloat16)
        put_scr[pair] = pick.T.astype(jnp.bfloat16)
        share_scr[pair] = jnp.sum(shares, axis=1, keepdims=True)

    for pair in range(pair_count):
        load(pair).wait()
    for e in range(1, experts):
        for which in range(3):
            weight_copy(e, which).start()

    @pl.loop(0, pair_count)
    def _(pair):
        for part in range(2):
            columns = pl.ds(part * half, half)
            rows = jnp.dot(
                pick_scr[pair], x_scr[pair, :, columns], preferred_element_type=jnp.float32
            ).astype(jnp.bfloat16)
            for e in range(experts):
                h_scr[e, pl.ds(pl.multiple_of(pair * slots, slots), slots), columns] = rows[
                    e * slots : (e + 1) * slots
                ]

    tile, wide_tile = 256, 512

    @pl.loop(0, experts)
    def _(e):
        def wait(which):
            pltpu.make_async_copy(
                weights[0][which].at[0], buffers[which].at[e], w_sems.at[which, e]
            ).wait()

        wait(0)
        wait(1)
        for begin in range(0, hid_scr.shape[1], tile):
            columns = pl.ds(begin, tile)
            gate = jnp.dot(h_scr[e], gate_scr[e, :, columns], preferred_element_type=jnp.float32)
            up = jnp.dot(h_scr[e], up_scr[e, :, columns], preferred_element_type=jnp.float32)
            hid_scr[:, columns] = (gate / (1.0 + jnp.exp(-gate)) * up).astype(jnp.bfloat16)
        wait(2)
        for begin in range(0, width, wide_tile):
            columns = pl.ds(begin, wide_tile)
            rows = jnp.dot(hid_scr[...], down_scr[e, :, columns], preferred_element_type=jnp.float32)
            for pair in range(pair_count):
                slot_rows = pl.ds(pl.multiple_of(e * slots, slots), slots)
                y_scr[pair, slot_rows, columns] = (
                    rows[pair * slots : (pair + 1) * slots] * share_scr[pair, slot_rows, :]
                ).astype(jnp.bfloat16)

    for pair in reversed(range(pair_count)):
        for part in range(2):
            columns = pl.ds(part * half, half)
            x_scr[pair, :, columns] = jnp.dot(
                put_scr[pair], y_scr[pair, :, columns], preferred_element_type=jnp.float32
            ).astype(jnp.bfloat16)
        store(pair).start()
    for pair in range(pair_count):
        store(pair).wait()


def run_experts(info, told, own, sib, pieces, outers, behind=()):
    width, hidden = own[0].shape[1:]
    experts = 4
    pair_count = 2 * len(outers)
    pair_tokens = pieces[0].shape[0]
    slots = 3 * pair_tokens * TOPK // (2 * experts * CHIPS)
    pair_rows = experts * slots
    rows = pair_count * slots
    return pl.pallas_call(
        functools.partial(expert_kernel, outers, len(told), len(behind)),
        out_shape=[jax.ShapeDtypeStruct((pair_tokens, width), jnp.bfloat16)] * pair_count,
        in_specs=[pl.BlockSpec(memory_space=pltpu.SMEM)] + [ANY] * (6 + len(told) + len(pieces) + len(behind)),
        out_specs=[ANY] * pair_count,
        scratch_shapes=[
            pltpu.VMEM((2 * pair_count, TOLD_ROWS, told[0].shape[1]), jnp.bfloat16),
            pltpu.VMEM((pair_count, pair_rows, pair_tokens), jnp.bfloat16),
            pltpu.VMEM((pair_count, pair_tokens, pair_rows), jnp.bfloat16),
            pltpu.VMEM((pair_count, pair_rows, 1), jnp.float32),
            pltpu.VMEM((pair_count, pair_tokens, width), jnp.bfloat16),
            pltpu.VMEM((experts, rows, width), jnp.bfloat16),
            pltpu.VMEM((rows, hidden), jnp.bfloat16),
            pltpu.VMEM((pair_count, pair_rows, width), jnp.bfloat16),
            pltpu.VMEM((experts, width, hidden), jnp.bfloat16),
            pltpu.VMEM((experts, width, hidden), jnp.bfloat16),
            pltpu.VMEM((experts, hidden, width), jnp.bfloat16),
            pltpu.SemaphoreType.DMA((2 * pair_count,)),
            pltpu.SemaphoreType.DMA((pair_count,)),
            pltpu.SemaphoreType.DMA((pair_count,)),
            pltpu.SemaphoreType.DMA((3, experts)),
        ],
        compiler_params=pltpu.CompilerParams(vmem_limit_bytes=VMEM_LIMIT),
        cost_estimate=pl.CostEstimate(
            flops=6 * experts * rows * width * hidden,
            bytes_accessed=56 << 20,
            transcendentals=experts * rows * hidden,
        ),
        name="experts_%d" % outers[0],
    )(info, *told, *own, *sib, *pieces, *behind)


def told_routes(routes, route_gates, experts_all):
    tokens = routes.shape[0]
    share = route_gates / jnp.sum(route_gates, axis=1, keepdims=True)
    named = (routes[:, :, None] == jnp.arange(experts_all, dtype=jnp.int32)).astype(jnp.float32)
    hits = jnp.sum(named, axis=1)
    order = jnp.arange(tokens)
    earlier = (order[None, :] < order[:, None]).astype(jnp.bfloat16)
    rank = jnp.dot(earlier, hits.astype(jnp.bfloat16), preferred_element_type=jnp.float32)
    rank = jnp.sum(named * rank[:, None, :], axis=2)
    high = share.astype(jnp.bfloat16)
    left = share - high.astype(jnp.float32)
    mid = left.astype(jnp.bfloat16)
    low = (left - mid.astype(jnp.float32)).astype(jnp.bfloat16)
    first = jnp.concatenate([routes.astype(jnp.bfloat16).T, rank.astype(jnp.bfloat16).T, high.T, mid.T], axis=1)
    return jnp.concatenate([first, jnp.pad(low.T, ((0, 0), (0, 3 * tokens)))], axis=0)


def in_order(c, mine, theirs):
    return jnp.where(
        c == 0, jnp.concatenate([mine, theirs], axis=0), jnp.concatenate([theirs, mine], axis=0)
    )


def body(
    queries,
    key_vectors,
    value_vectors,
    residual,
    out_weight,
    norm_gain,
    routes,
    route_gates,
    w_gate,
    w_up,
    w_down,
):
    me = lax.axis_index("seq")
    c = me % CORES
    x = me // CORES % SIDE
    y = me // (CORES * SIDE)
    info = jnp.stack([y, x, c]).astype(jnp.int32)
    tokens, width = residual.shape
    experts_all = w_gate.shape[0] * lax.axis_size("seq")

    kv_half = key_vectors.shape[1] // 2
    q_half = queries.shape[1] // 2

    def half_of(array, which, size):
        return lax.dynamic_slice_in_dim(array, which * size, size, axis=1)

    def kv_of(which):
        k, v = (half_of(a, which, kv_half) for a in (key_vectors, value_vectors))
        d = HEAD_DIM
        return jnp.concatenate([k[:, :d], v[:, :d], k[:, d:], v[:, d:]], axis=1)

    kv_send, q_send = together(kv_of(1 - c), half_of(queries, 1 - c, q_half))
    kv = in_order(c, kv_of(c), to_sibling(kv_send))
    q_got = to_sibling(q_send)
    told = told_routes(routes, route_gates, experts_all)
    kv = jnp.concatenate([kv, told], axis=0)

    weight = lax.all_gather(out_weight, "seq", axis=0, tiled=True)
    own = (w_gate, w_up, w_down)

    line = gather_near(kv, 1)
    wide = gather_wide(line)
    q = in_order(c, half_of(queries, c, q_half), q_got)
    sums = attend(info, q, line, (0,))
    wide_done, far = gather_far(wide, sums[:1])
    *sends, _ = together(*own, wide_done)
    sib = [to_sibling(w) for w in sends]
    sums = attend(info, q, wide, (1, 2), sums)
    attended = attend(info, q, far, (3,), sums)
    keep, send = project(info, attended, weight, sib)
    stream, normed = norm(keep, to_sibling(send), residual, norm_gain)
    told_line, told_wide, told_far = line, wide, far
    line = gather_near(normed, 2)
    wide = gather_wide(line)
    partial = run_experts(info, told_line, own, sib, line, (0,))
    _, far = gather_far(wide, partial[:1])
    partial += run_experts(info, told_wide, own, sib, wide, (1, 2))
    partial += run_experts(info, told_far, own, sib, far, (3,), partial[2:3])
    expert_sum = scatter_grid(partial)
    layer_out = (stream.astype(jnp.float32) + expert_sum).astype(jnp.bfloat16)
    return (stream, layer_out)


def solution(mesh):
    in_specs = (
        P(("dp", "seq"), None),
        P(("dp", "seq"), None),
        P(("dp", "seq"), None),
        P(("dp", "seq"), None),
        P("seq", None),
        P(),
        P(("dp", "seq"), None),
        P(("dp", "seq"), None),
        P("seq", None, None),
        P("seq", None, None),
        P("seq", None, None),
    )
    out_specs = (P(("dp", "seq"), None), P(("dp", "seq"), None))
    return jax.shard_map(body, mesh=mesh, in_specs=in_specs, out_specs=out_specs, check_vma=False)
```

```python
import functools

import jax
import jax.numpy as jnp
from jax import lax
from jax.experimental import pallas as pl
from jax.experimental.pallas import tpu as pltpu
from jax.sharding import PartitionSpec as P

HEADS = 32
KV_HEADS = 4
HEAD_DIM = 128
TOPK = 8
SIDE = 4
CHIPS = SIDE * SIDE
CORES = 2
OFFSETS = (0, -1, 1, 2)
TOLD_ROWS = 16
LOG2E = 1.4426950408889634
ANY = pl.BlockSpec(memory_space=pl.ANY)
WHOLE = pl.BlockSpec(memory_space=pltpu.VMEM)
MIB = 1024 * 1024
VMEM_LIMIT = 60 * MIB


def ring_pairs(stage, step):
    pairs = []
    for y in range(SIDE):
        for x in range(SIDE):
            for c in range(CORES):
                dy, dx = (step, 0) if stage != c else (0, step)
                source = (y * SIDE + x) * CORES + c
                target = ((y + dy) % SIDE * SIDE + (x + dx) % SIDE) * CORES + c
                pairs.append((source, target))
    return pairs


def along(value, stage, step):
    return lax.ppermute(value, "seq", ring_pairs(stage, step))


def to_sibling(value):
    devices = CHIPS * CORES
    return lax.ppermute(value, "seq", [(d, d ^ 1) for d in range(devices)])


def together(*values):
    return lax.optimization_barrier(values)


def rearrange(sources, plan, name, behind=()):
    width = sources[0].shape[1]

    def kernel(*refs):
        ins, outs = refs[: len(sources)], refs[len(sources) + len(behind) :]
        for out, parts in zip(outs, plan):
            at = 0
            for source, begin, rows in parts:
                out[at : at + rows, :] = ins[source][begin : begin + rows, :]
                at += rows

    rows_out = [sum(rows for _, _, rows in parts) for parts in plan]
    return pl.pallas_call(
        kernel,
        out_shape=[jax.ShapeDtypeStruct((rows, width), sources[0].dtype) for rows in rows_out],
        in_specs=[WHOLE] * len(sources) + [ANY] * len(behind),
        out_specs=[WHOLE] * len(plan),
        compiler_params=pltpu.CompilerParams(vmem_limit_bytes=24 * MIB),
        cost_estimate=pl.CostEstimate(
            flops=0, bytes_accessed=4 * width * sum(rows_out), transcendentals=0
        ),
        name=name,
    )(*sources, *behind)


def gather_near(block, pieces):
    rows = block.shape[0]
    got = [along(block, 0, step) for step in (1, -1, 2)]
    each = SIDE // pieces
    plan = [[(i, 0, rows) for i in range(p * each, (p + 1) * each)] for p in range(pieces)]
    return rearrange([block, *got], plan, "line")


def gather_wide(line):
    before = [along(piece, 1, 1) for piece in line]
    after = [along(piece, 1, -1) for piece in line]
    return before + after


def gather_far(wide, behind):
    if len(wide) == 4:
        low, high, *_ = together(wide[0], wide[3], *behind)
    else:
        half = wide[0].shape[0] // 2
        low, high = rearrange(wide, [[(0, 0, half)], [(1, half, half)]], "halves", behind)
    return low, [along(low, 1, 1), along(high, 1, -1)]


def locate(lines, pieces, at, inner, rows):
    if pieces == lines:
        return at, inner * rows
    return 2 * at + inner // 2, (inner % 2) * rows


def add(*terms):
    return functools.reduce(jnp.add, [term.astype(jnp.float32) for term in terms])


def add_kernel(groups, *refs):
    terms, outs = refs[: sum(groups)], refs[sum(groups) :]
    each = len(outs) // len(groups)
    for at, count in enumerate(groups):
        first = sum(groups[:at])
        total = add(*(term[...] for term in terms[first : first + count]))
        rows = total.shape[0] // each
        for i in range(each):
            outs[at * each + i][...] = total[i * rows : (i + 1) * rows].astype(jnp.bfloat16)


def add_groups(groups, parts, *terms):
    rows, width = terms[0].shape
    shape = jax.ShapeDtypeStruct((rows // parts, width), jnp.bfloat16)
    return pl.pallas_call(
        functools.partial(add_kernel, groups),
        out_shape=[shape] * (len(groups) * parts),
        in_specs=[WHOLE] * len(terms),
        out_specs=[WHOLE] * (len(groups) * parts),
        compiler_params=pltpu.CompilerParams(vmem_limit_bytes=24 * MIB),
        cost_estimate=pl.CostEstimate(
            flops=len(terms) * rows * width,
            bytes_accessed=2 * (len(terms) + len(groups)) * rows * width,
            transcendentals=0,
        ),
        name="add_groups",
    )(*terms)


def scatter_grid(halves):
    own_low, own_high, before_low, before_high, after_low, after_high, far_low, far_high = halves
    early_high, early_low = along(after_high, 1, 1), along(before_low, 1, -1)
    far_low, far_high, early_high, early_low = together(far_low, far_high, early_high, early_low)
    got_low, got_high = along(far_low, 1, 1), along(far_high, 1, -1)
    low, high = add_groups((2, 2), 1, after_low, got_low, before_high, got_high)
    late_low, late_high = along(low, 1, 1), along(high, 1, -1)
    own, before, after, far = add_groups(
        (3, 3), 2, own_low, late_low, early_low, own_high, early_high, late_high
    )
    return add(own, along(after, 0, 1), along(before, 0, -1), along(far, 0, 2))


def norm_kernel(keep_ref, got_ref, residual_ref, gain_ref, stream_ref, normed_ref):
    attn_sum = keep_ref[...] + got_ref[...].astype(jnp.float32)
    stream = (residual_ref[...].astype(jnp.float32) + attn_sum).astype(jnp.bfloat16)
    stream_ref[...] = stream
    stream = stream.astype(jnp.float32)
    mean = jnp.mean(stream * stream, axis=1, keepdims=True)
    normed_ref[...] = (stream * lax.rsqrt(mean + 1e-06) * gain_ref[...]).astype(jnp.bfloat16)


def norm(keep, got, residual, gain):
    tokens, width = residual.shape
    whole = jax.ShapeDtypeStruct((tokens, width), jnp.bfloat16)
    return pl.pallas_call(
        norm_kernel,
        out_shape=(whole, whole),
        in_specs=[WHOLE] * 4,
        out_specs=[WHOLE] * 2,
        compiler_params=pltpu.CompilerParams(vmem_limit_bytes=16 * MIB),
        cost_estimate=pl.CostEstimate(
            flops=8 * tokens * width, bytes_accessed=14 * tokens * width, transcendentals=tokens
        ),
        name="norm",
    )(keep, got, residual, gain[None, :])


def attend_kernel(outers, count, first, last, info, q_ref, *refs):
    pieces, refs = refs[:count], refs[count:]
    if not first:
        top_in, total_in, acc_in, *refs = refs
    if last:
        out_ref, *refs = refs
    else:
        top_out, total_out, acc_out, *refs = refs
    kv_scr, turned, top, total, acc, sems = refs
    y, x, c = info[0], info[1], info[2]
    chip = y * SIDE + x
    block = 256
    group = pl.program_id(0) // 2

    def copies(at):
        made = []
        for inner in range(SIDE):
            piece, row = locate(len(outers), count, at, inner, block + TOLD_ROWS)
            source = pieces[piece].at[pl.ds(row, block)]
            target = kv_scr.at[at, pl.ds(inner * block, block)]
            made.append(pltpu.make_async_copy(source, target, sems.at[at, inner]))
        return made

    def turn(at):
        columns = pl.ds(pl.multiple_of((2 * group + 1) * HEAD_DIM, HEAD_DIM), HEAD_DIM)
        for inner in range(SIDE):
            rows = pl.ds(inner * block, block)
            value = kv_scr[at, rows, columns].astype(jnp.float32)
            turned[at, :, inner * block : (inner + 1) * block] = value.T.astype(jnp.bfloat16)

    @pl.when(pl.program_id(0) == 0)
    def _():
        for at in range(len(outers)):
            for copy in copies(at):
                copy.start()
        for at in range(len(outers)):
            for copy in copies(at):
                copy.wait()
            turn(at)

    @pl.when(pl.program_id(0) == 2)
    def _():
        for at in range(len(outers)):
            turn(at)

    scale = HEAD_DIM ** (-0.5) * LOG2E
    heads = q_ref.shape[1] // HEAD_DIM
    q = jnp.concatenate(
        [q_ref[:, h * HEAD_DIM : (h + 1) * HEAD_DIM] for h in range(heads)], axis=0
    )
    if not first:
        top[...], total[...], acc[...] = top_in[0], total_in[0], acc_in[0]
    else:
        top[...] = jnp.full(top.shape, -1e30, jnp.float32)
        total[...] = jnp.zeros(total.shape, jnp.float32)
        acc[...] = jnp.zeros(acc.shape, jnp.float32)

    def step(at, key):
        columns = pl.ds(pl.multiple_of(2 * group * HEAD_DIM, HEAD_DIM), HEAD_DIM)
        s = (
            lax.dot_general(
                kv_scr[at, :, columns],
                q,
                (((1,), (1,)), ((), ())),
                preferred_element_type=jnp.float32,
            )
            * scale
        )
        if key is not None:
            query = lax.broadcasted_iota(jnp.int32, (1, s.shape[1]), 1) % block + chip * block
            s = jnp.where(key <= query, s, -1e30)
        old = top[...]
        new = jnp.maximum(old, jnp.max(s, axis=0, keepdims=True))
        p = jnp.exp2(s - new)
        shrink = jnp.exp2(old - new)
        top[...] = new
        total[...] = total[...] * shrink + jnp.sum(p, axis=0, keepdims=True)
        acc[...] = acc[...] * shrink + jnp.dot(
            turned[at], p.astype(jnp.bfloat16), preferred_element_type=jnp.float32
        )

    @pl.loop(0, len(outers))
    def _(at):
        offset = jnp.where(at == 0, OFFSETS[outers[0]], OFFSETS[outers[-1]])
        line_y = lax.rem(y + offset + SIDE, SIDE)
        line_x = lax.rem(x + offset + SIDE, SIDE)
        least = jnp.where(c == 0, line_y * SIDE, line_x)
        most = jnp.where(c == 0, line_y * SIDE + SIDE - 1, CHIPS - SIDE + line_x)

        @pl.when(most < chip)
        def _():
            step(at, None)

        @pl.when((most >= chip) & (least <= chip))
        def _():
            homes = []
            for inner in range(SIDE):
                other = OFFSETS[inner] + SIDE
                home = jnp.where(
                    c == 0,
                    line_y * SIDE + lax.rem(x + other, SIDE),
                    lax.rem(y + other, SIDE) * SIDE + line_x,
                )
                homes.append(lax.broadcasted_iota(jnp.int32, (block, 1), 0) + home * block)
            step(at, jnp.concatenate(homes, axis=0))

    if last:
        out = (acc[...] / total[...]).T.astype(jnp.bfloat16)
        for h in range(heads):
            out_ref[:, h * HEAD_DIM : (h + 1) * HEAD_DIM] = out[h * block : (h + 1) * block]
    else:
        top_out[0], total_out[0], acc_out[0] = top[...], total[...], acc[...]


def attend(info, q, pieces, outers, carried=()):
    tokens, width = q.shape
    steps = 4
    at_once = width // steps
    first, last = outers[0] == 0, outers[-1] == 3
    columns = at_once // HEAD_DIM * tokens
    q_spec = pl.BlockSpec((tokens, at_once), lambda i, info: (0, i))
    shapes = [(1, columns), (1, columns), (HEAD_DIM, columns)]
    specs = [pl.BlockSpec((1, *shape), lambda i, info: (i, 0, 0)) for shape in shapes]
    sums = [jax.ShapeDtypeStruct((steps, *shape), jnp.float32) for shape in shapes]
    keys = SIDE * tokens
    lines = len(outers)
    return pl.pallas_call(
        functools.partial(attend_kernel, outers, len(pieces), first, last),
        out_shape=jax.ShapeDtypeStruct((tokens, width), jnp.bfloat16) if last else sums,
        grid_spec=pltpu.PrefetchScalarGridSpec(
            num_scalar_prefetch=1,
            grid=(steps,),
            in_specs=[q_spec] + [ANY] * len(pieces) + specs[: len(carried)],
            out_specs=q_spec if last else specs,
            scratch_shapes=[
                pltpu.VMEM((lines, keys, 4 * HEAD_DIM), jnp.bfloat16),
                pltpu.VMEM((lines, HEAD_DIM, keys), jnp.bfloat16),
                *(pltpu.VMEM(shape, jnp.float32) for shape in shapes),
                pltpu.SemaphoreType.DMA((lines, SIDE)),
            ],
        ),
        compiler_params=pltpu.CompilerParams(vmem_limit_bytes=VMEM_LIMIT),
        cost_estimate=pl.CostEstimate(
            flops=4 * tokens * width * keys * lines,
            bytes_accessed=6 << 20,
            transcendentals=tokens * width * keys * lines // HEAD_DIM,
        ),
        name="attend_%d" % outers[0],
    )(info, q, *pieces, *carried)


def project_kernel(info, *refs):
    part, w_ref = refs[:2]
    keep_ref, send_ref, w_scr, sems = refs[-4:]
    c = info[2]
    depth, width = part.shape[1], w_ref.shape[1]
    tokens = keep_ref.shape[0]

    own = pl.ds(pl.multiple_of(c * tokens, tokens), tokens)
    other = pl.ds(pl.multiple_of((1 - c) * tokens, tokens), tokens)
    tiles = w_scr.shape[0]
    tile = width // tiles

    def copy_of(i):
        source = w_ref.at[pl.ds(pl.multiple_of(c * depth, depth), depth), pl.ds(i * tile, tile)]
        return pltpu.make_async_copy(source, w_scr.at[i], sems.at[i])

    for i in range(tiles):
        copy_of(i).start()
    turned = jnp.concatenate([part[own, :], part[other, :]], axis=0)
    for i in range(tiles):
        copy_of(i).wait()
        product = jnp.dot(turned, w_scr[i], preferred_element_type=jnp.float32)
        columns = pl.ds(i * tile, tile)
        keep_ref[:, columns] = product[:tokens]
        send_ref[:, columns] = product[tokens:].astype(send_ref.dtype)


def project(info, attended, weight, behind):
    width = weight.shape[1]
    tokens, depth = attended.shape[0] // CORES, attended.shape[1]
    tiles = 4
    vmem = pl.BlockSpec(memory_space=pltpu.VMEM)
    return pl.pallas_call(
        project_kernel,
        out_shape=(
            jax.ShapeDtypeStruct((tokens, width), jnp.float32),
            jax.ShapeDtypeStruct((tokens, width), jnp.bfloat16),
        ),
        in_specs=[pl.BlockSpec(memory_space=pltpu.SMEM), vmem, ANY] + [ANY] * len(behind),
        out_specs=(vmem, vmem),
        scratch_shapes=[
            pltpu.VMEM((tiles, depth, width // tiles), jnp.bfloat16),
            pltpu.SemaphoreType.DMA((tiles,)),
        ],
        compiler_params=pltpu.CompilerParams(vmem_limit_bytes=24 * MIB),
        cost_estimate=pl.CostEstimate(
            flops=4 * tokens * width * depth, bytes_accessed=12 << 20, transcendentals=0
        ),
        name="project",
    )(info, attended, weight, *behind)


def expert_kernel(outers, told_count, behind, info, *refs):
    pair_count = 2 * len(outers)
    count = pair_count
    told, refs = refs[:told_count], refs[told_count:]
    weights, refs = (refs[:3], refs[3:6]), refs[6:]
    pieces, refs = refs[:count], refs[count + behind :]
    outs, refs = refs[:pair_count], refs[pair_count:]
    told_scr, pick_scr, put_scr, share_scr, x_scr, h_scr, hid_scr, y_scr = refs[:8]
    gate_scr, up_scr, down_scr, told_sems, in_sems, out_sems, w_sems = refs[8:]
    _, pair_rows, pair_tokens = pick_scr.shape
    experts = 4
    slots = pair_rows // experts
    block = pair_tokens // 2
    width = x_scr.shape[2]
    half = width // 2
    buffers = (gate_scr, up_scr, down_scr)

    def weight_copy(e, which):
        source = weights[e // 2][which].at[e % 2]
        return pltpu.make_async_copy(source, buffers[which].at[e], w_sems.at[which, e])

    def load(pair):
        return pltpu.make_async_copy(pieces[pair], x_scr.at[pair], in_sems.at[pair])

    def store(pair):
        return pltpu.make_async_copy(x_scr.at[pair], outs[pair], out_sems.at[pair])

    told_copies = []
    for at in range(len(outers)):
        for inner in range(SIDE):
            piece, row = locate(len(outers), told_count, at, inner, CORES * block + TOLD_ROWS)
            number = at * SIDE + inner
            told_copies.append(
                pltpu.make_async_copy(
                    told[piece].at[pl.ds(row + CORES * block, TOLD_ROWS)],
                    told_scr.at[number],
                    told_sems.at[number],
                )
            )
    for copy in told_copies:
        copy.start()
    for pair in range(pair_count):
        load(pair).start()
    for which in range(3):
        weight_copy(0, which).start()
    for copy in told_copies:
        copy.wait()

    first_expert = (info[0] * SIDE + info[1]) * experts
    own_first = 2 * info[2]

    def routes_of(number, at):
        rows = told_scr[number].astype(jnp.float32)
        expert, rank, high, mid = (rows[:TOPK, i * block : (i + 1) * block] for i in range(4))
        share = high + mid + rows[TOPK:, :block]
        local = expert.astype(jnp.int32) - first_expert
        here = (local >= 0) & (local < experts)
        local = local - own_first
        local = jnp.where(local < 0, local + experts, local)
        row = local * slots + at * (slots // 2) + rank.astype(jnp.int32)
        return jnp.where(here, row, -1), share

    @pl.loop(0, pair_count)
    def _(pair):
        row, share = zip(*(routes_of(2 * pair + at, at) for at in range(2)))
        row, share = jnp.concatenate(row, axis=1), jnp.concatenate(share, axis=1)
        slot = lax.broadcasted_iota(jnp.int32, (pair_rows, pair_tokens), 0)
        pick = jnp.zeros(slot.shape, jnp.float32)
        shares = jnp.zeros(slot.shape, jnp.float32)
        for r in range(TOPK):
            match = row[r : r + 1, :] == slot
            pick = jnp.where(match, 1.0, pick)
            shares = jnp.where(match, share[r : r + 1, :], shares)
        pick_scr[pair] = pick.astype(jnp.bfloat16)
        put_scr[pair] = pick.T.astype(jnp.bfloat16)
        share_scr[pair] = jnp.sum(shares, axis=1, keepdims=True)

    for pair in range(pair_count):
        load(pair).wait()
    for e in range(1, experts):
        for which in range(3):
            weight_copy(e, which).start()

    @pl.loop(0, pair_count)
    def _(pair):
        for part in range(2):
            columns = pl.ds(part * half, half)
            rows = jnp.dot(
                pick_scr[pair], x_scr[pair, :, columns], preferred_element_type=jnp.float32
            ).astype(jnp.bfloat16)
            for e in range(experts):
                h_scr[e, pl.ds(pl.multiple_of(pair * slots, slots), slots), columns] = rows[
                    e * slots : (e + 1) * slots
                ]

    tile, wide_tile = 256, 512

    @pl.loop(0, experts)
    def _(e):
        def wait(which):
            pltpu.make_async_copy(
                weights[0][which].at[0], buffers[which].at[e], w_sems.at[which, e]
            ).wait()

        wait(0)
        wait(1)
        for begin in range(0, hid_scr.shape[1], tile):
            columns = pl.ds(begin, tile)
            gate = jnp.dot(h_scr[e], gate_scr[e, :, columns], preferred_element_type=jnp.float32)
            up = jnp.dot(h_scr[e], up_scr[e, :, columns], preferred_element_type=jnp.float32)
            hid_scr[:, columns] = (gate / (1.0 + jnp.exp(-gate)) * up).astype(jnp.bfloat16)
        wait(2)
        for begin in range(0, width, wide_tile):
            columns = pl.ds(begin, wide_tile)
            rows = jnp.dot(hid_scr[...], down_scr[e, :, columns], preferred_element_type=jnp.float32)
            for pair in range(pair_count):
                slot_rows = pl.ds(pl.multiple_of(e * slots, slots), slots)
                y_scr[pair, slot_rows, columns] = (
                    rows[pair * slots : (pair + 1) * slots] * share_scr[pair, slot_rows, :]
                ).astype(jnp.bfloat16)

    for pair in reversed(range(pair_count)):
        for part in range(2):
            columns = pl.ds(part * half, half)
            x_scr[pair, :, columns] = jnp.dot(
                put_scr[pair], y_scr[pair, :, columns], preferred_element_type=jnp.float32
            ).astype(jnp.bfloat16)
        store(pair).start()
    for pair in range(pair_count):
        store(pair).wait()


def run_experts(info, told, own, sib, pieces, outers, behind=()):
    width, hidden = own[0].shape[1:]
    experts = 4
    pair_count = 2 * len(outers)
    pair_tokens = pieces[0].shape[0]
    slots = 3 * pair_tokens * TOPK // (2 * experts * CHIPS)
    pair_rows = experts * slots
    rows = pair_count * slots
    return pl.pallas_call(
        functools.partial(expert_kernel, outers, len(told), len(behind)),
        out_shape=[jax.ShapeDtypeStruct((pair_tokens, width), jnp.bfloat16)] * pair_count,
        in_specs=[pl.BlockSpec(memory_space=pltpu.SMEM)] + [ANY] * (6 + len(told) + len(pieces) + len(behind)),
        out_specs=[ANY] * pair_count,
        scratch_shapes=[
            pltpu.VMEM((2 * pair_count, TOLD_ROWS, told[0].shape[1]), jnp.bfloat16),
            pltpu.VMEM((pair_count, pair_rows, pair_tokens), jnp.bfloat16),
            pltpu.VMEM((pair_count, pair_tokens, pair_rows), jnp.bfloat16),
            pltpu.VMEM((pair_count, pair_rows, 1), jnp.float32),
            pltpu.VMEM((pair_count, pair_tokens, width), jnp.bfloat16),
            pltpu.VMEM((experts, rows, width), jnp.bfloat16),
            pltpu.VMEM((rows, hidden), jnp.bfloat16),
            pltpu.VMEM((pair_count, pair_rows, width), jnp.bfloat16),
            pltpu.VMEM((experts, width, hidden), jnp.bfloat16),
            pltpu.VMEM((experts, width, hidden), jnp.bfloat16),
            pltpu.VMEM((experts, hidden, width), jnp.bfloat16),
            pltpu.SemaphoreType.DMA((2 * pair_count,)),
            pltpu.SemaphoreType.DMA((pair_count,)),
            pltpu.SemaphoreType.DMA((pair_count,)),
            pltpu.SemaphoreType.DMA((3, experts)),
        ],
        compiler_params=pltpu.CompilerParams(vmem_limit_bytes=(42 + 3 * pair_count) * MIB),
        cost_estimate=pl.CostEstimate(
            flops=6 * experts * rows * width * hidden,
            bytes_accessed=56 << 20,
            transcendentals=experts * rows * hidden,
        ),
        name="experts_%d" % outers[0],
    )(info, *told, *own, *sib, *pieces, *behind)


def told_routes(routes, route_gates, experts_all):
    tokens = routes.shape[0]
    share = route_gates / jnp.sum(route_gates, axis=1, keepdims=True)
    named = (routes[:, :, None] == jnp.arange(experts_all, dtype=jnp.int32)).astype(jnp.float32)
    hits = jnp.sum(named, axis=1)
    order = jnp.arange(tokens)
    earlier = (order[None, :] < order[:, None]).astype(jnp.bfloat16)
    rank = jnp.dot(earlier, hits.astype(jnp.bfloat16), preferred_element_type=jnp.float32)
    rank = jnp.sum(named * rank[:, None, :], axis=2)
    high = share.astype(jnp.bfloat16)
    left = share - high.astype(jnp.float32)
    mid = left.astype(jnp.bfloat16)
    low = (left - mid.astype(jnp.float32)).astype(jnp.bfloat16)
    first = jnp.concatenate([routes.astype(jnp.bfloat16).T, rank.astype(jnp.bfloat16).T, high.T, mid.T], axis=1)
    return jnp.concatenate([first, jnp.pad(low.T, ((0, 0), (0, 3 * tokens)))], axis=0)


def in_order(c, mine, theirs):
    return jnp.where(
        c == 0, jnp.concatenate([mine, theirs], axis=0), jnp.concatenate([theirs, mine], axis=0)
    )


def body(
    queries,
    key_vectors,
    value_vectors,
    residual,
    out_weight,
    norm_gain,
    routes,
    route_gates,
    w_gate,
    w_up,
    w_down,
):
    me = lax.axis_index("seq")
    c = me % CORES
    x = me // CORES % SIDE
    y = me // (CORES * SIDE)
    info = jnp.stack([y, x, c]).astype(jnp.int32)
    tokens, width = residual.shape
    experts_all = w_gate.shape[0] * lax.axis_size("seq")

    kv_half = key_vectors.shape[1] // 2
    q_half = queries.shape[1] // 2

    def half_of(array, which, size):
        return lax.dynamic_slice_in_dim(array, which * size, size, axis=1)

    def kv_of(which):
        k, v = (half_of(a, which, kv_half) for a in (key_vectors, value_vectors))
        d = HEAD_DIM
        return jnp.concatenate([k[:, :d], v[:, :d], k[:, d:], v[:, d:]], axis=1)

    kv_send, q_send = together(kv_of(1 - c), half_of(queries, 1 - c, q_half))
    kv = in_order(c, kv_of(c), to_sibling(kv_send))
    q_got = to_sibling(q_send)
    told = told_routes(routes, route_gates, experts_all)
    kv = jnp.concatenate([kv, told], axis=0)

    weight = lax.all_gather(out_weight, "seq", axis=0, tiled=True)
    own = (w_gate, w_up, w_down)

    line = gather_near(kv, 1)
    wide = gather_wide(line)
    q = in_order(c, half_of(queries, c, q_half), q_got)
    sums = attend(info, q, line, (0,))
    wide_done, far = gather_far(wide, sums[:1])
    *sends, _ = together(*own, wide_done)
    sib = [to_sibling(w) for w in sends]
    sums = attend(info, q, wide, (1, 2), sums)
    attended = attend(info, q, far, (3,), sums)
    keep, send = project(info, attended, weight, sib)
    stream, normed = norm(keep, to_sibling(send), residual, norm_gain)
    told_line, told_wide, told_far = line, wide, far
    line = gather_near(normed, 2)
    wide = gather_wide(line)
    partial = run_experts(info, told_line, own, sib, line, (0,))
    _, far = gather_far(wide, partial[:1])
    partial += run_experts(info, told_wide, own, sib, wide, (1, 2))
    partial += run_experts(info, told_far, own, sib, far, (3,), partial[2:3])
    expert_sum = scatter_grid(partial)
    layer_out = (stream.astype(jnp.float32) + expert_sum).astype(jnp.bfloat16)
    return (stream, layer_out)


def solution(mesh):
    in_specs = (
        P(("dp", "seq"), None),
        P(("dp", "seq"), None),
        P(("dp", "seq"), None),
        P(("dp", "seq"), None),
        P("seq", None),
        P(),
        P(("dp", "seq"), None),
        P(("dp", "seq"), None),
        P("seq", None, None),
        P("seq", None, None),
        P("seq", None, None),
    )
    out_specs = (P(("dp", "seq"), None), P(("dp", "seq"), None))
    return jax.shard_map(body, mesh=mesh, in_specs=in_specs, out_specs=out_specs, check_vma=False)
```

```python
import functools

import jax
import jax.numpy as jnp
from jax import lax
from jax.experimental import pallas as pl
from jax.experimental.pallas import tpu as pltpu
from jax.sharding import PartitionSpec as P

HEADS = 32
KV_HEADS = 4
HEAD_DIM = 128
TOPK = 8
SIDE = 4
CHIPS = SIDE * SIDE
CORES = 2
OFFSETS = (0, -1, 1, 2)
TOLD_ROWS = 16
LOG2E = 1.4426950408889634
ANY = pl.BlockSpec(memory_space=pl.ANY)
WHOLE = pl.BlockSpec(memory_space=pltpu.VMEM)
MIB = 1024 * 1024
VMEM_LIMIT = 60 * MIB


def ring_pairs(stage, step):
    pairs = []
    for y in range(SIDE):
        for x in range(SIDE):
            for c in range(CORES):
                dy, dx = (step, 0) if stage != c else (0, step)
                source = (y * SIDE + x) * CORES + c
                target = ((y + dy) % SIDE * SIDE + (x + dx) % SIDE) * CORES + c
                pairs.append((source, target))
    return pairs


def along(value, stage, step):
    return lax.ppermute(value, "seq", ring_pairs(stage, step))


def to_sibling(value):
    devices = CHIPS * CORES
    return lax.ppermute(value, "seq", [(d, d ^ 1) for d in range(devices)])


def together(*values):
    return lax.optimization_barrier(values)


def rearrange(sources, plan, name, behind=()):
    width = sources[0].shape[1]

    def kernel(*refs):
        ins, outs = refs[: len(sources)], refs[len(sources) + len(behind) :]
        for out, parts in zip(outs, plan):
            at = 0
            for source, begin, rows in parts:
                out[at : at + rows, :] = ins[source][begin : begin + rows, :]
                at += rows

    rows_out = [sum(rows for _, _, rows in parts) for parts in plan]
    return pl.pallas_call(
        kernel,
        out_shape=[jax.ShapeDtypeStruct((rows, width), sources[0].dtype) for rows in rows_out],
        in_specs=[WHOLE] * len(sources) + [ANY] * len(behind),
        out_specs=[WHOLE] * len(plan),
        compiler_params=pltpu.CompilerParams(vmem_limit_bytes=24 * MIB),
        cost_estimate=pl.CostEstimate(
            flops=0, bytes_accessed=4 * width * sum(rows_out), transcendentals=0
        ),
        name=name,
    )(*sources, *behind)


def gather_near(block, pieces):
    rows = block.shape[0]
    got = [along(block, 0, step) for step in (1, -1, 2)]
    each = SIDE // pieces
    plan = [[(i, 0, rows) for i in range(p * each, (p + 1) * each)] for p in range(pieces)]
    return rearrange([block, *got], plan, "line")


def gather_wide(line):
    before = [along(piece, 1, 1) for piece in line]
    after = [along(piece, 1, -1) for piece in line]
    return before + after


def gather_far(wide, behind):
    if len(wide) == 4:
        low, high, *_ = together(wide[0], wide[3], *behind)
    else:
        half = wide[0].shape[0] // 2
        low, high = rearrange(wide, [[(0, 0, half)], [(1, half, half)]], "halves", behind)
    return low, [along(low, 1, 1), along(high, 1, -1)]


def locate(lines, pieces, at, inner, rows):
    if pieces == lines:
        return at, inner * rows
    return 2 * at + inner // 2, (inner % 2) * rows


def add(*terms):
    return functools.reduce(jnp.add, [term.astype(jnp.float32) for term in terms])


def add_kernel(groups, *refs):
    terms, outs = refs[: sum(groups)], refs[sum(groups) :]
    each = len(outs) // len(groups)
    for at, count in enumerate(groups):
        first = sum(groups[:at])
        total = add(*(term[...] for term in terms[first : first + count]))
        rows = total.shape[0] // each
        for i in range(each):
            outs[at * each + i][...] = total[i * rows : (i + 1) * rows].astype(jnp.bfloat16)


def add_groups(groups, parts, *terms):
    rows, width = terms[0].shape
    shape = jax.ShapeDtypeStruct((rows // parts, width), jnp.bfloat16)
    return pl.pallas_call(
        functools.partial(add_kernel, groups),
        out_shape=[shape] * (len(groups) * parts),
        in_specs=[WHOLE] * len(terms),
        out_specs=[WHOLE] * (len(groups) * parts),
        compiler_params=pltpu.CompilerParams(vmem_limit_bytes=24 * MIB),
        cost_estimate=pl.CostEstimate(
            flops=len(terms) * rows * width,
            bytes_accessed=2 * (len(terms) + len(groups)) * rows * width,
            transcendentals=0,
        ),
        name="add_groups",
    )(*terms)


def scatter_grid(halves):
    own_low, own_high, before_low, before_high, after_low, after_high, far_low, far_high = halves
    early_high, early_low = along(after_high, 1, 1), along(before_low, 1, -1)
    far_low, far_high, early_high, early_low = together(far_low, far_high, early_high, early_low)
    got_low, got_high = along(far_low, 1, 1), along(far_high, 1, -1)
    low, high = add_groups((2, 2), 1, after_low, got_low, before_high, got_high)
    late_low, late_high = along(low, 1, 1), along(high, 1, -1)
    own, before, after, far = add_groups(
        (3, 3), 2, own_low, late_low, early_low, own_high, early_high, late_high
    )
    return add(own, along(after, 0, 1), along(before, 0, -1), along(far, 0, 2))


def norm_kernel(keep_ref, got_ref, residual_ref, gain_ref, stream_ref, normed_ref):
    attn_sum = keep_ref[...] + got_ref[...].astype(jnp.float32)
    stream = (residual_ref[...].astype(jnp.float32) + attn_sum).astype(jnp.bfloat16)
    stream_ref[...] = stream
    stream = stream.astype(jnp.float32)
    mean = jnp.mean(stream * stream, axis=1, keepdims=True)
    normed_ref[...] = (stream * lax.rsqrt(mean + 1e-06) * gain_ref[...]).astype(jnp.bfloat16)


def norm(keep, got, residual, gain):
    tokens, width = residual.shape
    whole = jax.ShapeDtypeStruct((tokens, width), jnp.bfloat16)
    return pl.pallas_call(
        norm_kernel,
        out_shape=(whole, whole),
        in_specs=[WHOLE] * 4,
        out_specs=[WHOLE] * 2,
        compiler_params=pltpu.CompilerParams(vmem_limit_bytes=16 * MIB),
        cost_estimate=pl.CostEstimate(
            flops=8 * tokens * width, bytes_accessed=14 * tokens * width, transcendentals=tokens
        ),
        name="norm",
    )(keep, got, residual, gain[None, :])


def attend_kernel(outers, count, first, last, info, q_ref, *refs):
    pieces, refs = refs[:count], refs[count:]
    if not first:
        top_in, total_in, acc_in, *refs = refs
    if last:
        out_ref, *refs = refs
    else:
        top_out, total_out, acc_out, *refs = refs
    kv_scr, turned, top, total, acc, sems = refs
    y, x, c = info[0], info[1], info[2]
    chip = y * SIDE + x
    block = 256
    group = pl.program_id(0) // 2

    def copies(at):
        made = []
        for inner in range(SIDE):
            piece, row = locate(len(outers), count, at, inner, block + TOLD_ROWS)
            source = pieces[piece].at[pl.ds(row, block)]
            target = kv_scr.at[at, pl.ds(inner * block, block)]
            made.append(pltpu.make_async_copy(source, target, sems.at[at, inner]))
        return made

    def turn(at):
        columns = pl.ds(pl.multiple_of((2 * group + 1) * HEAD_DIM, HEAD_DIM), HEAD_DIM)
        for inner in range(SIDE):
            rows = pl.ds(inner * block, block)
            value = kv_scr[at, rows, columns].astype(jnp.float32)
            turned[at, :, inner * block : (inner + 1) * block] = value.T.astype(jnp.bfloat16)

    @pl.when(pl.program_id(0) == 0)
    def _():
        for at in range(len(outers)):
            for copy in copies(at):
                copy.start()
        for at in range(len(outers)):
            for copy in copies(at):
                copy.wait()
            turn(at)

    @pl.when(pl.program_id(0) == 2)
    def _():
        for at in range(len(outers)):
            turn(at)

    scale = HEAD_DIM ** (-0.5) * LOG2E
    heads = q_ref.shape[1] // HEAD_DIM
    q = jnp.concatenate(
        [q_ref[:, h * HEAD_DIM : (h + 1) * HEAD_DIM] for h in range(heads)], axis=0
    )
    if not first:
        top[...], total[...], acc[...] = top_in[0], total_in[0], acc_in[0]
    else:
        top[...] = jnp.full(top.shape, -1e30, jnp.float32)
        total[...] = jnp.zeros(total.shape, jnp.float32)
        acc[...] = jnp.zeros(acc.shape, jnp.float32)

    def step(at, key):
        columns = pl.ds(pl.multiple_of(2 * group * HEAD_DIM, HEAD_DIM), HEAD_DIM)
        s = (
            lax.dot_general(
                kv_scr[at, :, columns],
                q,
                (((1,), (1,)), ((), ())),
                preferred_element_type=jnp.float32,
            )
            * scale
        )
        if key is not None:
            query = lax.broadcasted_iota(jnp.int32, (1, s.shape[1]), 1) % block + chip * block
            s = jnp.where(key <= query, s, -1e30)
        old = top[...]
        new = jnp.maximum(old, jnp.max(s, axis=0, keepdims=True))
        p = jnp.exp2(s - new)
        shrink = jnp.exp2(old - new)
        top[...] = new
        total[...] = total[...] * shrink + jnp.sum(p, axis=0, keepdims=True)
        acc[...] = acc[...] * shrink + jnp.dot(
            turned[at], p.astype(jnp.bfloat16), preferred_element_type=jnp.float32
        )

    @pl.loop(0, len(outers))
    def _(at):
        offset = jnp.where(at == 0, OFFSETS[outers[0]], OFFSETS[outers[-1]])
        line_y = lax.rem(y + offset + SIDE, SIDE)
        line_x = lax.rem(x + offset + SIDE, SIDE)
        least = jnp.where(c == 0, line_y * SIDE, line_x)
        most = jnp.where(c == 0, line_y * SIDE + SIDE - 1, CHIPS - SIDE + line_x)

        @pl.when(most < chip)
        def _():
            step(at, None)

        @pl.when((most >= chip) & (least <= chip))
        def _():
            homes = []
            for inner in range(SIDE):
                other = OFFSETS[inner] + SIDE
                home = jnp.where(
                    c == 0,
                    line_y * SIDE + lax.rem(x + other, SIDE),
                    lax.rem(y + other, SIDE) * SIDE + line_x,
                )
                homes.append(lax.broadcasted_iota(jnp.int32, (block, 1), 0) + home * block)
            step(at, jnp.concatenate(homes, axis=0))

    if last:
        out = (acc[...] / total[...]).T.astype(jnp.bfloat16)
        for h in range(heads):
            out_ref[:, h * HEAD_DIM : (h + 1) * HEAD_DIM] = out[h * block : (h + 1) * block]
    else:
        top_out[0], total_out[0], acc_out[0] = top[...], total[...], acc[...]


def attend(info, q, pieces, outers, carried=()):
    tokens, width = q.shape
    steps = 4
    at_once = width // steps
    first, last = outers[0] == 0, outers[-1] == 3
    columns = at_once // HEAD_DIM * tokens
    q_spec = pl.BlockSpec((tokens, at_once), lambda i, info: (0, i))
    shapes = [(1, columns), (1, columns), (HEAD_DIM, columns)]
    specs = [pl.BlockSpec((1, *shape), lambda i, info: (i, 0, 0)) for shape in shapes]
    sums = [jax.ShapeDtypeStruct((steps, *shape), jnp.float32) for shape in shapes]
    keys = SIDE * tokens
    lines = len(outers)
    return pl.pallas_call(
        functools.partial(attend_kernel, outers, len(pieces), first, last),
        out_shape=jax.ShapeDtypeStruct((tokens, width), jnp.bfloat16) if last else sums,
        grid_spec=pltpu.PrefetchScalarGridSpec(
            num_scalar_prefetch=1,
            grid=(steps,),
            in_specs=[q_spec] + [ANY] * len(pieces) + specs[: len(carried)],
            out_specs=q_spec if last else specs,
            scratch_shapes=[
                pltpu.VMEM((lines, keys, 4 * HEAD_DIM), jnp.bfloat16),
                pltpu.VMEM((lines, HEAD_DIM, keys), jnp.bfloat16),
                *(pltpu.VMEM(shape, jnp.float32) for shape in shapes),
                pltpu.SemaphoreType.DMA((lines, SIDE)),
            ],
        ),
        compiler_params=pltpu.CompilerParams(vmem_limit_bytes=VMEM_LIMIT),
        cost_estimate=pl.CostEstimate(
            flops=4 * tokens * width * keys * lines,
            bytes_accessed=6 << 20,
            transcendentals=tokens * width * keys * lines // HEAD_DIM,
        ),
        name="attend_%d" % outers[0],
    )(info, q, *pieces, *carried)


def project_kernel(info, *refs):
    part, w_ref = refs[:2]
    keep_ref, send_ref, w_scr, sems = refs[-4:]
    c = info[2]
    depth, width = part.shape[1], w_ref.shape[1]
    tokens = keep_ref.shape[0]

    own = pl.ds(pl.multiple_of(c * tokens, tokens), tokens)
    other = pl.ds(pl.multiple_of((1 - c) * tokens, tokens), tokens)
    tiles = w_scr.shape[0]
    tile = width // tiles

    def copy_of(i):
        source = w_ref.at[pl.ds(pl.multiple_of(c * depth, depth), depth), pl.ds(i * tile, tile)]
        return pltpu.make_async_copy(source, w_scr.at[i], sems.at[i])

    for i in range(tiles):
        copy_of(i).start()
    turned = jnp.concatenate([part[own, :], part[other, :]], axis=0)
    for i in range(tiles):
        copy_of(i).wait()
        product = jnp.dot(turned, w_scr[i], preferred_element_type=jnp.float32)
        columns = pl.ds(i * tile, tile)
        keep_ref[:, columns] = product[:tokens]
        send_ref[:, columns] = product[tokens:].astype(send_ref.dtype)


def project(info, attended, weight, behind):
    width = weight.shape[1]
    tokens, depth = attended.shape[0] // CORES, attended.shape[1]
    tiles = 8
    vmem = pl.BlockSpec(memory_space=pltpu.VMEM)
    return pl.pallas_call(
        project_kernel,
        out_shape=(
            jax.ShapeDtypeStruct((tokens, width), jnp.float32),
            jax.ShapeDtypeStruct((tokens, width), jnp.bfloat16),
        ),
        in_specs=[pl.BlockSpec(memory_space=pltpu.SMEM), vmem, ANY] + [ANY] * len(behind),
        out_specs=(vmem, vmem),
        scratch_shapes=[
            pltpu.VMEM((tiles, depth, width // tiles), jnp.bfloat16),
            pltpu.SemaphoreType.DMA((tiles,)),
        ],
        compiler_params=pltpu.CompilerParams(vmem_limit_bytes=24 * MIB),
        cost_estimate=pl.CostEstimate(
            flops=4 * tokens * width * depth, bytes_accessed=12 << 20, transcendentals=0
        ),
        name="project",
    )(info, attended, weight, *behind)


def expert_kernel(outers, told_count, behind, info, *refs):
    pair_count = 2 * len(outers)
    count = pair_count
    told, refs = refs[:told_count], refs[told_count:]
    weights, refs = (refs[:3], refs[3:6]), refs[6:]
    pieces, refs = refs[:count], refs[count + behind :]
    outs, refs = refs[:pair_count], refs[pair_count:]
    told_scr, pick_scr, put_scr, share_scr, x_scr, h_scr, hid_scr, y_scr = refs[:8]
    gate_scr, up_scr, down_scr, told_sems, in_sems, out_sems, w_sems = refs[8:]
    _, pair_rows, pair_tokens = pick_scr.shape
    experts = 4
    slots = pair_rows // experts
    block = pair_tokens // 2
    width = x_scr.shape[2]
    half = width // 2
    buffers = (gate_scr, up_scr, down_scr)

    def weight_copy(e, which):
        source = weights[e // 2][which].at[e % 2]
        return pltpu.make_async_copy(source, buffers[which].at[e], w_sems.at[which, e])

    def load(pair):
        return pltpu.make_async_copy(pieces[pair], x_scr.at[pair], in_sems.at[pair])

    def store(pair):
        return pltpu.make_async_copy(x_scr.at[pair], outs[pair], out_sems.at[pair])

    told_copies = []
    for at in range(len(outers)):
        for inner in range(SIDE):
            piece, row = locate(len(outers), told_count, at, inner, CORES * block + TOLD_ROWS)
            number = at * SIDE + inner
            told_copies.append(
                pltpu.make_async_copy(
                    told[piece].at[pl.ds(row + CORES * block, TOLD_ROWS)],
                    told_scr.at[number],
                    told_sems.at[number],
                )
            )
    for copy in told_copies:
        copy.start()
    for pair in range(pair_count):
        load(pair).start()
    for e in range(2):
        for which in range(3):
            weight_copy(e, which).start()
    for copy in told_copies:
        copy.wait()

    first_expert = (info[0] * SIDE + info[1]) * experts
    own_first = 2 * info[2]

    def routes_of(number, at):
        rows = told_scr[number].astype(jnp.float32)
        expert, rank, high, mid = (rows[:TOPK, i * block : (i + 1) * block] for i in range(4))
        share = high + mid + rows[TOPK:, :block]
        local = expert.astype(jnp.int32) - first_expert
        here = (local >= 0) & (local < experts)
        local = local - own_first
        local = jnp.where(local < 0, local + experts, local)
        row = local * slots + at * (slots // 2) + rank.astype(jnp.int32)
        return jnp.where(here, row, -1), share

    @pl.loop(0, pair_count)
    def _(pair):
        row, share = zip(*(routes_of(2 * pair + at, at) for at in range(2)))
        row, share = jnp.concatenate(row, axis=1), jnp.concatenate(share, axis=1)
        slot = lax.broadcasted_iota(jnp.int32, (pair_rows, pair_tokens), 0)
        pick = jnp.zeros(slot.shape, jnp.float32)
        shares = jnp.zeros(slot.shape, jnp.float32)
        for r in range(TOPK):
            match = row[r : r + 1, :] == slot
            pick = jnp.where(match, 1.0, pick)
            shares = jnp.where(match, share[r : r + 1, :], shares)
        pick_scr[pair] = pick.astype(jnp.bfloat16)
        put_scr[pair] = pick.T.astype(jnp.bfloat16)
        share_scr[pair] = jnp.sum(shares, axis=1, keepdims=True)

    for pair in range(pair_count):
        load(pair).wait()
    for e in range(2, experts):
        for which in range(3):
            weight_copy(e, which).start()

    @pl.loop(0, pair_count)
    def _(pair):
        for part in range(2):
            columns = pl.ds(part * half, half)
            rows = jnp.dot(
                pick_scr[pair], x_scr[pair, :, columns], preferred_element_type=jnp.float32
            ).astype(jnp.bfloat16)
            for e in range(experts):
                h_scr[e, pl.ds(pl.multiple_of(pair * slots, slots), slots), columns] = rows[
                    e * slots : (e + 1) * slots
                ]

    tile, wide_tile = 256, 512

    @pl.loop(0, experts)
    def _(e):
        def wait(which):
            pltpu.make_async_copy(
                weights[0][which].at[0], buffers[which].at[e], w_sems.at[which, e]
            ).wait()

        wait(0)
        wait(1)
        for begin in range(0, hid_scr.shape[1], tile):
            columns = pl.ds(begin, tile)
            gate = jnp.dot(h_scr[e], gate_scr[e, :, columns], preferred_element_type=jnp.float32)
            up = jnp.dot(h_scr[e], up_scr[e, :, columns], preferred_element_type=jnp.float32)
            hid_scr[:, columns] = (gate / (1.0 + jnp.exp(-gate)) * up).astype(jnp.bfloat16)
        wait(2)
        for begin in range(0, width, wide_tile):
            columns = pl.ds(begin, wide_tile)
            rows = jnp.dot(hid_scr[...], down_scr[e, :, columns], preferred_element_type=jnp.float32)
            for pair in range(pair_count):
                slot_rows = pl.ds(pl.multiple_of(e * slots, slots), slots)
                y_scr[pair, slot_rows, columns] = (
                    rows[pair * slots : (pair + 1) * slots] * share_scr[pair, slot_rows, :]
                ).astype(jnp.bfloat16)

    for pair in reversed(range(pair_count)):
        for part in range(2):
            columns = pl.ds(part * half, half)
            x_scr[pair, :, columns] = jnp.dot(
                put_scr[pair], y_scr[pair, :, columns], preferred_element_type=jnp.float32
            ).astype(jnp.bfloat16)
        store(pair).start()
    for pair in range(pair_count):
        store(pair).wait()


def run_experts(info, told, own, sib, pieces, outers, behind=()):
    width, hidden = own[0].shape[1:]
    experts = 4
    pair_count = 2 * len(outers)
    pair_tokens = pieces[0].shape[0]
    slots = 3 * pair_tokens * TOPK // (2 * experts * CHIPS)
    pair_rows = experts * slots
    rows = pair_count * slots
    return pl.pallas_call(
        functools.partial(expert_kernel, outers, len(told), len(behind)),
        out_shape=[jax.ShapeDtypeStruct((pair_tokens, width), jnp.bfloat16)] * pair_count,
        in_specs=[pl.BlockSpec(memory_space=pltpu.SMEM)] + [ANY] * (6 + len(told) + len(pieces) + len(behind)),
        out_specs=[ANY] * pair_count,
        scratch_shapes=[
            pltpu.VMEM((2 * pair_count, TOLD_ROWS, told[0].shape[1]), jnp.bfloat16),
            pltpu.VMEM((pair_count, pair_rows, pair_tokens), jnp.bfloat16),
            pltpu.VMEM((pair_count, pair_tokens, pair_rows), jnp.bfloat16),
            pltpu.VMEM((pair_count, pair_rows, 1), jnp.float32),
            pltpu.VMEM((pair_count, pair_tokens, width), jnp.bfloat16),
            pltpu.VMEM((experts, rows, width), jnp.bfloat16),
            pltpu.VMEM((rows, hidden), jnp.bfloat16),
            pltpu.VMEM((pair_count, pair_rows, width), jnp.bfloat16),
            pltpu.VMEM((experts, width, hidden), jnp.bfloat16),
            pltpu.VMEM((experts, width, hidden), jnp.bfloat16),
            pltpu.VMEM((experts, hidden, width), jnp.bfloat16),
            pltpu.SemaphoreType.DMA((2 * pair_count,)),
            pltpu.SemaphoreType.DMA((pair_count,)),
            pltpu.SemaphoreType.DMA((pair_count,)),
            pltpu.SemaphoreType.DMA((3, experts)),
        ],
        compiler_params=pltpu.CompilerParams(vmem_limit_bytes=(42 + 3 * pair_count) * MIB),
        cost_estimate=pl.CostEstimate(
            flops=6 * experts * rows * width * hidden,
            bytes_accessed=56 << 20,
            transcendentals=experts * rows * hidden,
        ),
        name="experts_%d" % outers[0],
    )(info, *told, *own, *sib, *pieces, *behind)


def told_routes(routes, route_gates, experts_all):
    tokens = routes.shape[0]
    share = route_gates / jnp.sum(route_gates, axis=1, keepdims=True)
    named = (routes[:, :, None] == jnp.arange(experts_all, dtype=jnp.int32)).astype(jnp.float32)
    hits = jnp.sum(named, axis=1)
    order = jnp.arange(tokens)
    earlier = (order[None, :] < order[:, None]).astype(jnp.bfloat16)
    rank = jnp.dot(earlier, hits.astype(jnp.bfloat16), preferred_element_type=jnp.float32)
    rank = jnp.sum(named * rank[:, None, :], axis=2)
    high = share.astype(jnp.bfloat16)
    left = share - high.astype(jnp.float32)
    mid = left.astype(jnp.bfloat16)
    low = (left - mid.astype(jnp.float32)).astype(jnp.bfloat16)
    first = jnp.concatenate([routes.astype(jnp.bfloat16).T, rank.astype(jnp.bfloat16).T, high.T, mid.T], axis=1)
    return jnp.concatenate([first, jnp.pad(low.T, ((0, 0), (0, 3 * tokens)))], axis=0)


def in_order(c, mine, theirs):
    return jnp.where(
        c == 0, jnp.concatenate([mine, theirs], axis=0), jnp.concatenate([theirs, mine], axis=0)
    )


def body(
    queries,
    key_vectors,
    value_vectors,
    residual,
    out_weight,
    norm_gain,
    routes,
    route_gates,
    w_gate,
    w_up,
    w_down,
):
    me = lax.axis_index("seq")
    c = me % CORES
    x = me // CORES % SIDE
    y = me // (CORES * SIDE)
    info = jnp.stack([y, x, c]).astype(jnp.int32)
    tokens, width = residual.shape
    experts_all = w_gate.shape[0] * lax.axis_size("seq")

    kv_half = key_vectors.shape[1] // 2
    q_half = queries.shape[1] // 2

    def half_of(array, which, size):
        return lax.dynamic_slice_in_dim(array, which * size, size, axis=1)

    def kv_of(which):
        k, v = (half_of(a, which, kv_half) for a in (key_vectors, value_vectors))
        d = HEAD_DIM
        return jnp.concatenate([k[:, :d], v[:, :d], k[:, d:], v[:, d:]], axis=1)

    kv_send, q_send = together(kv_of(1 - c), half_of(queries, 1 - c, q_half))
    kv = in_order(c, kv_of(c), to_sibling(kv_send))
    q_got = to_sibling(q_send)
    told = told_routes(routes, route_gates, experts_all)
    kv = jnp.concatenate([kv, told], axis=0)

    weight = lax.all_gather(out_weight, "seq", axis=0, tiled=True)
    own = (w_gate, w_up, w_down)

    line = gather_near(kv, 1)
    wide = gather_wide(line)
    q = in_order(c, half_of(queries, c, q_half), q_got)
    sums = attend(info, q, line, (0,))
    wide_done, far = gather_far(wide, sums[:1])
    *sends, _ = together(*own, wide_done)
    sib = [to_sibling(w) for w in sends]
    sums = attend(info, q, wide, (1, 2), sums)
    attended = attend(info, q, far, (3,), sums)
    keep, send = project(info, attended, weight, sib)
    stream, normed = norm(keep, to_sibling(send), residual, norm_gain)
    told_line, told_wide, told_far = line, wide, far
    line = gather_near(normed, 2)
    wide = gather_wide(line)
    partial = run_experts(info, told_line, own, sib, line, (0,))
    _, far = gather_far(wide, partial[:1])
    partial += run_experts(info, told_wide, own, sib, wide, (1, 2))
    partial += run_experts(info, told_far, own, sib, far, (3,), partial[2:3])
    expert_sum = scatter_grid(partial)
    layer_out = (stream.astype(jnp.float32) + expert_sum).astype(jnp.bfloat16)
    return (stream, layer_out)


def solution(mesh):
    in_specs = (
        P(("dp", "seq"), None),
        P(("dp", "seq"), None),
        P(("dp", "seq"), None),
        P(("dp", "seq"), None),
        P("seq", None),
        P(),
        P(("dp", "seq"), None),
        P(("dp", "seq"), None),
        P("seq", None, None),
        P("seq", None, None),
        P("seq", None, None),
    )
    out_specs = (P(("dp", "seq"), None), P(("dp", "seq"), None))
    return jax.shard_map(body, mesh=mesh, in_specs=in_specs, out_specs=out_specs, check_vma=False)
```

```python
import functools

import jax
import jax.numpy as jnp
from jax import lax
from jax.experimental import pallas as pl
from jax.experimental.pallas import tpu as pltpu
from jax.sharding import PartitionSpec as P

HEADS = 32
KV_HEADS = 4
HEAD_DIM = 128
TOPK = 8
SIDE = 4
CHIPS = SIDE * SIDE
CORES = 2
OFFSETS = (0, -1, 1, 2)
TOLD_ROWS = 16
LOG2E = 1.4426950408889634
ANY = pl.BlockSpec(memory_space=pl.ANY)
WHOLE = pl.BlockSpec(memory_space=pltpu.VMEM)
MIB = 1024 * 1024
VMEM_LIMIT = 60 * MIB


def ring_pairs(stage, step):
    pairs = []
    for y in range(SIDE):
        for x in range(SIDE):
            for c in range(CORES):
                dy, dx = (step, 0) if stage != c else (0, step)
                source = (y * SIDE + x) * CORES + c
                target = ((y + dy) % SIDE * SIDE + (x + dx) % SIDE) * CORES + c
                pairs.append((source, target))
    return pairs


def along(value, stage, step):
    return lax.ppermute(value, "seq", ring_pairs(stage, step))


def to_sibling(value):
    devices = CHIPS * CORES
    return lax.ppermute(value, "seq", [(d, d ^ 1) for d in range(devices)])


def together(*values):
    return lax.optimization_barrier(values)


def rearrange(sources, plan, name, behind=()):
    width = sources[0].shape[1]

    def kernel(*refs):
        ins, outs = refs[: len(sources)], refs[len(sources) + len(behind) :]
        for out, parts in zip(outs, plan):
            at = 0
            for source, begin, rows in parts:
                out[at : at + rows, :] = ins[source][begin : begin + rows, :]
                at += rows

    rows_out = [sum(rows for _, _, rows in parts) for parts in plan]
    return pl.pallas_call(
        kernel,
        out_shape=[jax.ShapeDtypeStruct((rows, width), sources[0].dtype) for rows in rows_out],
        in_specs=[WHOLE] * len(sources) + [ANY] * len(behind),
        out_specs=[WHOLE] * len(plan),
        compiler_params=pltpu.CompilerParams(vmem_limit_bytes=24 * MIB),
        cost_estimate=pl.CostEstimate(
            flops=0, bytes_accessed=4 * width * sum(rows_out), transcendentals=0
        ),
        name=name,
    )(*sources, *behind)


def gather_near(block, pieces):
    rows = block.shape[0]
    got = [along(block, 0, step) for step in (1, -1, 2)]
    each = SIDE // pieces
    plan = [[(i, 0, rows) for i in range(p * each, (p + 1) * each)] for p in range(pieces)]
    return rearrange([block, *got], plan, "line")


def gather_wide(line):
    before = [along(piece, 1, 1) for piece in line]
    after = [along(piece, 1, -1) for piece in line]
    return before + after


def gather_far(wide, behind):
    if len(wide) == 4:
        low, high, *_ = together(wide[0], wide[3], *behind)
    else:
        half = wide[0].shape[0] // 2
        low, high = rearrange(wide, [[(0, 0, half)], [(1, half, half)]], "halves", behind)
    return low, [along(low, 1, 1), along(high, 1, -1)]


def locate(lines, pieces, at, inner, rows):
    if pieces == lines:
        return at, inner * rows
    return 2 * at + inner // 2, (inner % 2) * rows


def add(*terms):
    return functools.reduce(jnp.add, [term.astype(jnp.float32) for term in terms])


def add_kernel(groups, *refs):
    terms, outs = refs[: sum(groups)], refs[sum(groups) :]
    each = len(outs) // len(groups)
    for at, count in enumerate(groups):
        first = sum(groups[:at])
        total = add(*(term[...] for term in terms[first : first + count]))
        rows = total.shape[0] // each
        for i in range(each):
            outs[at * each + i][...] = total[i * rows : (i + 1) * rows].astype(jnp.bfloat16)


def add_groups(groups, parts, *terms):
    rows, width = terms[0].shape
    shape = jax.ShapeDtypeStruct((rows // parts, width), jnp.bfloat16)
    return pl.pallas_call(
        functools.partial(add_kernel, groups),
        out_shape=[shape] * (len(groups) * parts),
        in_specs=[WHOLE] * len(terms),
        out_specs=[WHOLE] * (len(groups) * parts),
        compiler_params=pltpu.CompilerParams(vmem_limit_bytes=24 * MIB),
        cost_estimate=pl.CostEstimate(
            flops=len(terms) * rows * width,
            bytes_accessed=2 * (len(terms) + len(groups)) * rows * width,
            transcendentals=0,
        ),
        name="add_groups",
    )(*terms)


def scatter_grid(halves):
    own_low, own_high, before_low, before_high, after_low, after_high, far_low, far_high = halves
    early_high, early_low = along(after_high, 1, 1), along(before_low, 1, -1)
    far_low, far_high, early_high, early_low = together(far_low, far_high, early_high, early_low)
    got_low, got_high = along(far_low, 1, 1), along(far_high, 1, -1)
    low, high = add_groups((2, 2), 1, after_low, got_low, before_high, got_high)
    late_low, late_high = along(low, 1, 1), along(high, 1, -1)
    own, before, after, far = add_groups(
        (3, 3), 2, own_low, late_low, early_low, own_high, early_high, late_high
    )
    return add(own, along(after, 0, 1), along(before, 0, -1), along(far, 0, 2))


def norm_kernel(keep_ref, got_ref, residual_ref, gain_ref, stream_ref, normed_ref):
    attn_sum = keep_ref[...] + got_ref[...].astype(jnp.float32)
    stream = (residual_ref[...].astype(jnp.float32) + attn_sum).astype(jnp.bfloat16)
    stream_ref[...] = stream
    stream = stream.astype(jnp.float32)
    mean = jnp.mean(stream * stream, axis=1, keepdims=True)
    normed_ref[...] = (stream * lax.rsqrt(mean + 1e-06) * gain_ref[...]).astype(jnp.bfloat16)


def norm(keep, got, residual, gain):
    tokens, width = residual.shape
    whole = jax.ShapeDtypeStruct((tokens, width), jnp.bfloat16)
    return pl.pallas_call(
        norm_kernel,
        out_shape=(whole, whole),
        in_specs=[WHOLE] * 4,
        out_specs=[WHOLE] * 2,
        compiler_params=pltpu.CompilerParams(vmem_limit_bytes=16 * MIB),
        cost_estimate=pl.CostEstimate(
            flops=8 * tokens * width, bytes_accessed=14 * tokens * width, transcendentals=tokens
        ),
        name="norm",
    )(keep, got, residual, gain[None, :])


def attend_kernel(outers, count, first, last, info, q_ref, *refs):
    pieces, refs = refs[:count], refs[count:]
    if not first:
        top_in, total_in, acc_in, *refs = refs
    if last:
        out_ref, *refs = refs
    else:
        top_out, total_out, acc_out, *refs = refs
    kv_scr, turned, top, total, acc, sems = refs
    y, x, c = info[0], info[1], info[2]
    chip = y * SIDE + x
    block = 256
    group = pl.program_id(0) // 2

    def copies(at):
        made = []
        for inner in range(SIDE):
            piece, row = locate(len(outers), count, at, inner, block + TOLD_ROWS)
            source = pieces[piece].at[pl.ds(row, block)]
            target = kv_scr.at[at, pl.ds(inner * block, block)]
            made.append(pltpu.make_async_copy(source, target, sems.at[at, inner]))
        return made

    def turn(at):
        columns = pl.ds(pl.multiple_of((2 * group + 1) * HEAD_DIM, HEAD_DIM), HEAD_DIM)
        for inner in range(SIDE):
            rows = pl.ds(inner * block, block)
            value = kv_scr[at, rows, columns].astype(jnp.float32)
            turned[at, :, inner * block : (inner + 1) * block] = value.T.astype(jnp.bfloat16)

    @pl.when(pl.program_id(0) == 0)
    def _():
        for at in range(len(outers)):
            for copy in copies(at):
                copy.start()
        for at in range(len(outers)):
            for copy in copies(at):
                copy.wait()
            turn(at)

    @pl.when(pl.program_id(0) == 2)
    def _():
        for at in range(len(outers)):
            turn(at)

    scale = HEAD_DIM ** (-0.5) * LOG2E
    heads = q_ref.shape[1] // HEAD_DIM
    q = jnp.concatenate(
        [q_ref[:, h * HEAD_DIM : (h + 1) * HEAD_DIM] for h in range(heads)], axis=0
    )
    if not first:
        top[...], total[...], acc[...] = top_in[0], total_in[0], acc_in[0]
    else:
        top[...] = jnp.full(top.shape, -1e30, jnp.float32)
        total[...] = jnp.zeros(total.shape, jnp.float32)
        acc[...] = jnp.zeros(acc.shape, jnp.float32)

    def step(at, key):
        columns = pl.ds(pl.multiple_of(2 * group * HEAD_DIM, HEAD_DIM), HEAD_DIM)
        s = (
            lax.dot_general(
                kv_scr[at, :, columns],
                q,
                (((1,), (1,)), ((), ())),
                preferred_element_type=jnp.float32,
            )
            * scale
        )
        if key is not None:
            query = lax.broadcasted_iota(jnp.int32, (1, s.shape[1]), 1) % block + chip * block
            s = jnp.where(key <= query, s, -1e30)
        old = top[...]
        new = jnp.maximum(old, jnp.max(s, axis=0, keepdims=True))
        p = jnp.exp2(s - new)
        shrink = jnp.exp2(old - new)
        top[...] = new
        total[...] = total[...] * shrink + jnp.sum(p, axis=0, keepdims=True)
        acc[...] = acc[...] * shrink + jnp.dot(
            turned[at], p.astype(jnp.bfloat16), preferred_element_type=jnp.float32
        )

    @pl.loop(0, len(outers))
    def _(at):
        offset = jnp.where(at == 0, OFFSETS[outers[0]], OFFSETS[outers[-1]])
        line_y = lax.rem(y + offset + SIDE, SIDE)
        line_x = lax.rem(x + offset + SIDE, SIDE)
        least = jnp.where(c == 0, line_y * SIDE, line_x)
        most = jnp.where(c == 0, line_y * SIDE + SIDE - 1, CHIPS - SIDE + line_x)

        @pl.when(most < chip)
        def _():
            step(at, None)

        @pl.when((most >= chip) & (least <= chip))
        def _():
            homes = []
            for inner in range(SIDE):
                other = OFFSETS[inner] + SIDE
                home = jnp.where(
                    c == 0,
                    line_y * SIDE + lax.rem(x + other, SIDE),
                    lax.rem(y + other, SIDE) * SIDE + line_x,
                )
                homes.append(lax.broadcasted_iota(jnp.int32, (block, 1), 0) + home * block)
            step(at, jnp.concatenate(homes, axis=0))

    if last:
        out = (acc[...] / total[...]).T.astype(jnp.bfloat16)
        for h in range(heads):
            out_ref[:, h * HEAD_DIM : (h + 1) * HEAD_DIM] = out[h * block : (h + 1) * block]
    else:
        top_out[0], total_out[0], acc_out[0] = top[...], total[...], acc[...]


def attend(info, q, pieces, outers, carried=()):
    tokens, width = q.shape
    steps = 4
    at_once = width // steps
    first, last = outers[0] == 0, outers[-1] == 3
    columns = at_once // HEAD_DIM * tokens
    q_spec = pl.BlockSpec((tokens, at_once), lambda i, info: (0, i))
    shapes = [(1, columns), (1, columns), (HEAD_DIM, columns)]
    specs = [pl.BlockSpec((1, *shape), lambda i, info: (i, 0, 0)) for shape in shapes]
    sums = [jax.ShapeDtypeStruct((steps, *shape), jnp.float32) for shape in shapes]
    keys = SIDE * tokens
    lines = len(outers)
    return pl.pallas_call(
        functools.partial(attend_kernel, outers, len(pieces), first, last),
        out_shape=jax.ShapeDtypeStruct((tokens, width), jnp.bfloat16) if last else sums,
        grid_spec=pltpu.PrefetchScalarGridSpec(
            num_scalar_prefetch=1,
            grid=(steps,),
            in_specs=[q_spec] + [ANY] * len(pieces) + specs[: len(carried)],
            out_specs=q_spec if last else specs,
            scratch_shapes=[
                pltpu.VMEM((lines, keys, 4 * HEAD_DIM), jnp.bfloat16),
                pltpu.VMEM((lines, HEAD_DIM, keys), jnp.bfloat16),
                *(pltpu.VMEM(shape, jnp.float32) for shape in shapes),
                pltpu.SemaphoreType.DMA((lines, SIDE)),
            ],
        ),
        compiler_params=pltpu.CompilerParams(vmem_limit_bytes=VMEM_LIMIT),
        cost_estimate=pl.CostEstimate(
            flops=4 * tokens * width * keys * lines,
            bytes_accessed=6 << 20,
            transcendentals=tokens * width * keys * lines // HEAD_DIM,
        ),
        name="attend_%d" % outers[0],
    )(info, q, *pieces, *carried)


def project_kernel(info, *refs):
    part, w_ref = refs[:2]
    keep_ref, send_ref, w_scr, sems = refs[-4:]
    c = info[2]
    depth, width = part.shape[1], w_ref.shape[1]
    tokens = keep_ref.shape[0]

    own = pl.ds(pl.multiple_of(c * tokens, tokens), tokens)
    other = pl.ds(pl.multiple_of((1 - c) * tokens, tokens), tokens)
    tiles = w_scr.shape[0]
    tile = width // tiles

    def copy_of(i):
        source = w_ref.at[pl.ds(pl.multiple_of(c * depth, depth), depth), pl.ds(i * tile, tile)]
        return pltpu.make_async_copy(source, w_scr.at[i], sems.at[i])

    for i in range(tiles):
        copy_of(i).start()
    turned = jnp.concatenate([part[own, :], part[other, :]], axis=0)
    for i in range(tiles):
        copy_of(i).wait()
        product = jnp.dot(turned, w_scr[i], preferred_element_type=jnp.float32)
        columns = pl.ds(i * tile, tile)
        keep_ref[:, columns] = product[:tokens]
        send_ref[:, columns] = product[tokens:].astype(send_ref.dtype)


def project(info, attended, weight, behind):
    width = weight.shape[1]
    tokens, depth = attended.shape[0] // CORES, attended.shape[1]
    tiles = 8
    vmem = pl.BlockSpec(memory_space=pltpu.VMEM)
    return pl.pallas_call(
        project_kernel,
        out_shape=(
            jax.ShapeDtypeStruct((tokens, width), jnp.float32),
            jax.ShapeDtypeStruct((tokens, width), jnp.bfloat16),
        ),
        in_specs=[pl.BlockSpec(memory_space=pltpu.SMEM), vmem, ANY] + [ANY] * len(behind),
        out_specs=(vmem, vmem),
        scratch_shapes=[
            pltpu.VMEM((tiles, depth, width // tiles), jnp.bfloat16),
            pltpu.SemaphoreType.DMA((tiles,)),
        ],
        compiler_params=pltpu.CompilerParams(vmem_limit_bytes=24 * MIB),
        cost_estimate=pl.CostEstimate(
            flops=4 * tokens * width * depth, bytes_accessed=12 << 20, transcendentals=0
        ),
        name="project",
    )(info, attended, weight, *behind)


def expert_kernel(outers, told_count, behind, info, *refs):
    pair_count = 2 * len(outers)
    count = pair_count
    told, refs = refs[:told_count], refs[told_count:]
    weights, refs = (refs[:3], refs[3:6]), refs[6:]
    pieces, refs = refs[:count], refs[count + behind :]
    outs, refs = refs[:pair_count], refs[pair_count:]
    told_scr, pick_scr, put_scr, share_scr, x_scr, h_scr, hid_scr, y_scr = refs[:8]
    gate_scr, up_scr, down_scr, told_sems, in_sems, out_sems, w_sems = refs[8:]
    _, pair_rows, pair_tokens = pick_scr.shape
    experts = 4
    slots = pair_rows // experts
    block = pair_tokens // 2
    width = x_scr.shape[2]
    half = width // 2
    buffers = (gate_scr, up_scr, down_scr)

    def weight_copy(e, which):
        source = weights[e // 2][which].at[e % 2]
        return pltpu.make_async_copy(source, buffers[which].at[e], w_sems.at[which, e])

    def load(pair):
        return pltpu.make_async_copy(pieces[pair], x_scr.at[pair], in_sems.at[pair])

    def store(pair):
        return pltpu.make_async_copy(x_scr.at[pair], outs[pair], out_sems.at[pair])

    told_copies = []
    for at in range(len(outers)):
        for inner in range(SIDE):
            piece, row = locate(len(outers), told_count, at, inner, CORES * block + TOLD_ROWS)
            number = at * SIDE + inner
            told_copies.append(
                pltpu.make_async_copy(
                    told[piece].at[pl.ds(row + CORES * block, TOLD_ROWS)],
                    told_scr.at[number],
                    told_sems.at[number],
                )
            )
    for copy in told_copies:
        copy.start()
    for pair in range(pair_count):
        load(pair).start()
    for which in range(3):
        weight_copy(0, which).start()
    for copy in told_copies:
        copy.wait()

    first_expert = (info[0] * SIDE + info[1]) * experts
    own_first = 2 * info[2]

    def routes_of(number, at):
        rows = told_scr[number].astype(jnp.float32)
        expert, rank, high, mid = (rows[:TOPK, i * block : (i + 1) * block] for i in range(4))
        share = high + mid + rows[TOPK:, :block]
        local = expert.astype(jnp.int32) - first_expert
        here = (local >= 0) & (local < experts)
        local = local - own_first
        local = jnp.where(local < 0, local + experts, local)
        row = local * slots + at * (slots // 2) + rank.astype(jnp.int32)
        return jnp.where(here, row, -1), share

    @pl.loop(0, pair_count)
    def _(pair):
        row, share = zip(*(routes_of(2 * pair + at, at) for at in range(2)))
        row, share = jnp.concatenate(row, axis=1), jnp.concatenate(share, axis=1)
        slot = lax.broadcasted_iota(jnp.int32, (pair_rows, pair_tokens), 0)
        pick = jnp.zeros(slot.shape, jnp.float32)
        shares = jnp.zeros(slot.shape, jnp.float32)
        for r in range(TOPK):
            match = row[r : r + 1, :] == slot
            pick = jnp.where(match, 1.0, pick)
            shares = jnp.where(match, share[r : r + 1, :], shares)
        pick_scr[pair] = pick.astype(jnp.bfloat16)
        put_scr[pair] = pick.T.astype(jnp.bfloat16)
        share_scr[pair] = jnp.sum(shares, axis=1, keepdims=True)

    for pair in range(pair_count):
        load(pair).wait()
    for e in range(1, experts):
        for which in range(3):
            weight_copy(e, which).start()

    @pl.loop(0, pair_count)
    def _(pair):
        for part in range(2):
            columns = pl.ds(part * half, half)
            rows = jnp.dot(
                pick_scr[pair], x_scr[pair, :, columns], preferred_element_type=jnp.float32
            ).astype(jnp.bfloat16)
            for e in range(experts):
                h_scr[e, pl.ds(pl.multiple_of(pair * slots, slots), slots), columns] = rows[
                    e * slots : (e + 1) * slots
                ]

    tile, wide_tile = 256, 512

    @pl.loop(0, experts)
    def _(e):
        def wait(which):
            pltpu.make_async_copy(
                weights[0][which].at[0], buffers[which].at[e], w_sems.at[which, e]
            ).wait()

        wait(0)
        wait(1)
        for begin in range(0, hid_scr.shape[1], tile):
            columns = pl.ds(begin, tile)
            gate = jnp.dot(h_scr[e], gate_scr[e, :, columns], preferred_element_type=jnp.float32)
            up = jnp.dot(h_scr[e], up_scr[e, :, columns], preferred_element_type=jnp.float32)
            hid_scr[:, columns] = (gate / (1.0 + jnp.exp(-gate)) * up).astype(jnp.bfloat16)
        wait(2)
        for begin in range(0, width, wide_tile):
            columns = pl.ds(begin, wide_tile)
            rows = jnp.dot(hid_scr[...], down_scr[e, :, columns], preferred_element_type=jnp.float32)
            for pair in range(pair_count):
                slot_rows = pl.ds(pl.multiple_of(e * slots, slots), slots)
                y_scr[pair, slot_rows, columns] = (
                    rows[pair * slots : (pair + 1) * slots] * share_scr[pair, slot_rows, :]
                ).astype(jnp.bfloat16)

    for pair in reversed(range(pair_count)):
        for part in range(2):
            columns = pl.ds(part * half, half)
            x_scr[pair, :, columns] = jnp.dot(
                put_scr[pair], y_scr[pair, :, columns], preferred_element_type=jnp.float32
            ).astype(jnp.bfloat16)
        store(pair).start()
    for pair in range(pair_count):
        store(pair).wait()


def run_experts(info, told, own, sib, pieces, outers, behind=()):
    width, hidden = own[0].shape[1:]
    experts = 4
    pair_count = 2 * len(outers)
    pair_tokens = pieces[0].shape[0]
    slots = 3 * pair_tokens * TOPK // (2 * experts * CHIPS)
    pair_rows = experts * slots
    rows = pair_count * slots
    return pl.pallas_call(
        functools.partial(expert_kernel, outers, len(told), len(behind)),
        out_shape=[jax.ShapeDtypeStruct((pair_tokens, width), jnp.bfloat16)] * pair_count,
        in_specs=[pl.BlockSpec(memory_space=pltpu.SMEM)] + [ANY] * (6 + len(told) + len(pieces) + len(behind)),
        out_specs=[ANY] * pair_count,
        scratch_shapes=[
            pltpu.VMEM((2 * pair_count, TOLD_ROWS, told[0].shape[1]), jnp.bfloat16),
            pltpu.VMEM((pair_count, pair_rows, pair_tokens), jnp.bfloat16),
            pltpu.VMEM((pair_count, pair_tokens, pair_rows), jnp.bfloat16),
            pltpu.VMEM((pair_count, pair_rows, 1), jnp.float32),
            pltpu.VMEM((pair_count, pair_tokens, width), jnp.bfloat16),
            pltpu.VMEM((experts, rows, width), jnp.bfloat16),
            pltpu.VMEM((rows, hidden), jnp.bfloat16),
            pltpu.VMEM((pair_count, pair_rows, width), jnp.bfloat16),
            pltpu.VMEM((experts, width, hidden), jnp.bfloat16),
            pltpu.VMEM((experts, width, hidden), jnp.bfloat16),
            pltpu.VMEM((experts, hidden, width), jnp.bfloat16),
            pltpu.SemaphoreType.DMA((2 * pair_count,)),
            pltpu.SemaphoreType.DMA((pair_count,)),
            pltpu.SemaphoreType.DMA((pair_count,)),
            pltpu.SemaphoreType.DMA((3, experts)),
        ],
        compiler_params=pltpu.CompilerParams(vmem_limit_bytes=(42 + 3 * pair_count) * MIB),
        cost_estimate=pl.CostEstimate(
            flops=6 * experts * rows * width * hidden,
            bytes_accessed=56 << 20,
            transcendentals=experts * rows * hidden,
        ),
        name="experts_%d" % outers[0],
    )(info, *told, *own, *sib, *pieces, *behind)


def told_routes(routes, route_gates, experts_all):
    tokens = routes.shape[0]
    share = route_gates / jnp.sum(route_gates, axis=1, keepdims=True)
    named = (routes[:, :, None] == jnp.arange(experts_all, dtype=jnp.int32)).astype(jnp.float32)
    hits = jnp.sum(named, axis=1)
    order = jnp.arange(tokens)
    earlier = (order[None, :] < order[:, None]).astype(jnp.bfloat16)
    rank = jnp.dot(earlier, hits.astype(jnp.bfloat16), preferred_element_type=jnp.float32)
    rank = jnp.sum(named * rank[:, None, :], axis=2)
    high = share.astype(jnp.bfloat16)
    left = share - high.astype(jnp.float32)
    mid = left.astype(jnp.bfloat16)
    low = (left - mid.astype(jnp.float32)).astype(jnp.bfloat16)
    first = jnp.concatenate([routes.astype(jnp.bfloat16).T, rank.astype(jnp.bfloat16).T, high.T, mid.T], axis=1)
    return jnp.concatenate([first, jnp.pad(low.T, ((0, 0), (0, 3 * tokens)))], axis=0)


def in_order(c, mine, theirs):
    return jnp.where(
        c == 0, jnp.concatenate([mine, theirs], axis=0), jnp.concatenate([theirs, mine], axis=0)
    )


def body(
    queries,
    key_vectors,
    value_vectors,
    residual,
    out_weight,
    norm_gain,
    routes,
    route_gates,
    w_gate,
    w_up,
    w_down,
):
    me = lax.axis_index("seq")
    c = me % CORES
    x = me // CORES % SIDE
    y = me // (CORES * SIDE)
    info = jnp.stack([y, x, c]).astype(jnp.int32)
    tokens, width = residual.shape
    experts_all = w_gate.shape[0] * lax.axis_size("seq")

    kv_half = key_vectors.shape[1] // 2
    q_half = queries.shape[1] // 2

    def half_of(array, which, size):
        return lax.dynamic_slice_in_dim(array, which * size, size, axis=1)

    def kv_of(which):
        k, v = (half_of(a, which, kv_half) for a in (key_vectors, value_vectors))
        d = HEAD_DIM
        return jnp.concatenate([k[:, :d], v[:, :d], k[:, d:], v[:, d:]], axis=1)

    kv_send, q_send = together(kv_of(1 - c), half_of(queries, 1 - c, q_half))
    kv = in_order(c, kv_of(c), to_sibling(kv_send))
    q_got = to_sibling(q_send)
    told = told_routes(routes, route_gates, experts_all)
    kv = jnp.concatenate([kv, told], axis=0)

    weight = lax.all_gather(out_weight, "seq", axis=0, tiled=True)
    own = (w_gate, w_up, w_down)

    line = gather_near(kv, 1)
    wide = gather_wide(line)
    q = in_order(c, half_of(queries, c, q_half), q_got)
    sums = attend(info, q, line, (0,))
    wide_done, far = gather_far(wide, sums[:1])
    *sends, _ = together(*own, wide_done)
    sib = [to_sibling(w) for w in sends]
    sums = attend(info, q, wide, (1, 2), sums)
    attended = attend(info, q, far, (3,), sums)
    keep, send = project(info, attended, weight, sib)
    stream, normed = norm(keep, to_sibling(send), residual, norm_gain)
    told_line, told_wide, told_far = line, wide, far
    line = gather_near(normed, 2)
    wide = gather_wide(line)
    partial = run_experts(info, told_line, own, sib, line, (0,))
    _, far = gather_far(wide, partial[:1])
    partial += run_experts(info, told_wide, own, sib, wide, (1, 2))
    partial += run_experts(info, told_far, own, sib, far, (3,), partial[2:3])
    expert_sum = scatter_grid(partial)
    layer_out = (stream.astype(jnp.float32) + expert_sum).astype(jnp.bfloat16)
    return (stream, layer_out)


def solution(mesh):
    in_specs = (
        P(("dp", "seq"), None),
        P(("dp", "seq"), None),
        P(("dp", "seq"), None),
        P(("dp", "seq"), None),
        P("seq", None),
        P(),
        P(("dp", "seq"), None),
        P(("dp", "seq"), None),
        P("seq", None, None),
        P("seq", None, None),
        P("seq", None, None),
    )
    out_specs = (P(("dp", "seq"), None), P(("dp", "seq"), None))
    return jax.shard_map(body, mesh=mesh, in_specs=in_specs, out_specs=out_specs, check_vma=False)
```
